512 devices in a mesh: gz: 64 (over z, x), gx: 4 (over y_lo, core), gy: 2 (over y_hi).
Axes of the slice: x: 4, y: 4 (y_hi: 2, y_lo: 2; y = y_hi * 2 + y_lo), z: 16, core: 2. Of those that a mesh axis runs over, the one named last changes fastest.
Arguments:
- populations: float32 [19, 64, 256, 256], P(None, 'gz', 'gx', 'gy'), as said below
- solid_mask: int32 [64, 256, 256], P('gz', 'gx', 'gy'), may hold values from 0 to 1, as said below
- whirl_offsets: int32 [3, 2], replicated, may hold values from -3 to 3
- marker_cells: int32 [2, 64, 256], P(None, 'gz', ('gx', 'gy')), may hold values from -33 to 33, as said below
- marker_weights: float32 [2, 4, 64, 256], P(None, None, 'gz', ('gx', 'gy')), as said below
- pipe_velocity: float32 [3, 64, 256], P(None, 'gz', ('gx', 'gy')), may hold values from -0.2 to 0.2
Outputs:
- new_populations: float32 [19, 64, 256, 256], P(None, 'gz', 'gx', 'gy')
- velocity_field: float32 [3, 64, 256, 256], P(None, 'gz', 'gx', 'gy')
- marker_force: float32 [3, 64, 256], P(None, 'gz', ('gx', 'gy'))
The draws below stay inside these ranges and needn't reach their ends.
Inputs may be any that keep to these rules, and one draw needn't show every extreme that they name: `solid_mask`: 1 marks cells of the casing wall and of cuttings stuck to it; every cell on the grid's faces along the first and second cross-section dimensions is solid, and every cell within 38 cells of the grid's centre line along both is mud. `marker_cells`: every cycle traces the same octagon of radius 32 cells around the pipe axis, shifted by -1, 0 or 1 cell along each cross-section dimension, the same for all markers of a cycle. `marker_weights`: nonnegative kernel weights. `populations`: positive values near 1/3, 1/18 and 1/36 times a density near 1.
All inputs are finite; a program needn't handle non-finite values.
Results may differ from the reference program's by a relative error of at most 0.0003.
Values sent between devices are 32-bit elements; how exact they have to be, the bound alone decides.
A program may use at most 64 MiB of HBM per device.

```python
import jax
import jax.numpy as jnp

M = 256
PIPE_R = 32
STEPS = 3
NZ = 64
NX = 256
NY = 256


VELOCITIES = [(0, 0, 0), (1, 0, 0), (-1, 0, 0), (0, 1, 0), (0, -1, 0), (0, 0, 1), (0, 0, -1), (1, 1, 0), (-1, -1, 0), (1, -1, 0), (-1, 1, 0), (1, 0, 1), (-1, 0, -1), (1, 0, -1), (-1, 0, 1), (0, 1, 1), (0, -1, -1), (0, 1, -1), (0, -1, 1)]


LATTICE_WEIGHTS = [1.0 / 3.0] + [1.0 / 18.0] * 6 + [1.0 / 36.0] * 12


def draw_populations(key, part):
    first_key, second_key, third_key = jax.random.split(jax.random.fold_in(key, 11), 3)
    shape = (NZ, NX, NY)
    density = 1.0 + 0.1 * jax.random.uniform(first_key, shape, jnp.float32, -1.0, 1.0)
    velocity = 0.05 * jax.random.truncated_normal(second_key, -4.0, 4.0, (3,) + shape, jnp.float32)
    noise = jax.random.uniform(third_key, (19,) + shape, jnp.float32, -0.1, 0.1)
    squared = 1.5 * (velocity[0] * velocity[0] + velocity[1] * velocity[1] + velocity[2] * velocity[2])
    members = []
    for member in range(19):
        vector = VELOCITIES[member]
        projected = vector[0] * velocity[0] + vector[1] * velocity[1] + vector[2] * velocity[2]
        equilibrium = LATTICE_WEIGHTS[member] * density * (1.0 + 3.0 * projected + 4.5 * projected * projected - squared)
        members.append(equilibrium * (1.0 + noise[member]))
    return jnp.stack(members).astype(jnp.float32)


def draw_solid_mask(key, part):
    across = jnp.abs(2 * jnp.arange(NX, dtype=jnp.int32) - NX + 1) * 1024 // NX
    sideways = jnp.abs(2 * jnp.arange(NY, dtype=jnp.int32) - NY + 1) * 1024 // NY
    radius = across[:, None] * across[:, None] + sideways[None, :] * sideways[None, :]
    rough = jax.random.randint(jax.random.fold_in(key, 23), (NZ, NX, NY), 0, 160000, jnp.int32)
    return (radius[None] + rough > 883600).astype(jnp.int32)


def draw_marker_cells(key, part):
    corner = PIPE_R * 181 // 256
    vertex_x = jnp.array([PIPE_R, corner, 0, -corner, -PIPE_R, -corner, 0, corner, PIPE_R], jnp.int32)
    vertex_y = jnp.array([0, corner, PIPE_R, corner, 0, -corner, -PIPE_R, -corner, 0], jnp.int32)
    per_side = M // 8
    marker = jnp.arange(M, dtype=jnp.int32)
    side = marker // per_side
    offset = marker % per_side
    cycle_x = vertex_x[side] + (vertex_x[side + 1] - vertex_x[side]) * offset // per_side
    cycle_y = vertex_y[side] + (vertex_y[side + 1] - vertex_y[side]) * offset // per_side
    jitter = jax.random.randint(jax.random.fold_in(key, 37), (2, NZ, 1), -1, 2, jnp.int32)
    jitter = jitter.at[:, 0, :].set(1).at[:, 1, :].set(-1)
    return (jnp.stack([cycle_x, cycle_y])[:, None, :] + jitter).astype(jnp.int32)


def draw_marker_weights(key, part):
    fraction = jax.random.uniform(jax.random.fold_in(key, 41), (2, 1, NZ, M), jnp.float32)
    taps = jnp.arange(4, dtype=jnp.float32)[None, :, None, None]
    distance = jnp.abs(taps - 1.0 - fraction)
    return (0.25 * (1.0 + jnp.cos(0.5 * jnp.pi * distance))).astype(jnp.float32)


def place_ends(entries, rng, smallest, top_value):
    dims = entries.shape
    place = [jax.random.randint(jax.random.fold_in(rng, axis), (), 0, dims[axis]) for axis in range(len(dims))]
    entries = entries.at[tuple(place)].set(smallest)
    longest = dims.index(max(dims))
    place[longest] = (place[longest] + 1) % dims[longest]
    return entries.at[tuple(place)].set(top_value)


def levels(key, dims, cuts, least, high):
    def one(dim, blocks):
        heights = jax.random.uniform(jax.random.fold_in(jax.random.fold_in(key, 6), dim), (blocks,), jnp.float32, least / len(cuts), high / len(cuts))
        return jnp.repeat(jnp.exp(heights), dims[dim] // blocks).reshape((-1,) + (1,) * (len(dims) - dim - 1))

    factor_of = one(*cuts[0])
    for cut in cuts[1:]:
        factor_of = factor_of * one(*cut)
    return factor_of


def normal_values(key, extent, width, bound, shards=(), kind=jnp.bfloat16):
    gain = levels(key, extent, shards, -0.22, 0.18) if shards else 1.0
    values = jax.random.normal(key, extent, jnp.float32) * width * gain
    return jnp.minimum(jnp.maximum(values, -bound), bound).astype(kind)


def setup_inputs(seed: int = 0) -> dict:
    key_list = jax.random.split(jax.random.key(seed), 7)
    return {
        "populations": draw_populations(jax.random.fold_in(key_list[6], 71), 0),
        "solid_mask": draw_solid_mask(jax.random.fold_in(key_list[6], 71), 0),
        "whirl_offsets": place_ends(jax.random.randint(key_list[2], (STEPS, 2), -3, 4), jax.random.fold_in(key_list[2], 1), -3, 3).astype(jnp.int32),
        "marker_cells": draw_marker_cells(jax.random.fold_in(key_list[6], 71), 0),
        "marker_weights": draw_marker_weights(jax.random.fold_in(key_list[6], 71), 0),
        "pipe_velocity": normal_values(key_list[5], (3, NZ, M), 0.05, 0.2, ((1, 64), (2, 8)), jnp.float32),
    }


VELOCITIES = [(0, 0, 0), (1, 0, 0), (-1, 0, 0), (0, 1, 0), (0, -1, 0), (0, 0, 1), (0, 0, -1),
              (1, 1, 0), (-1, -1, 0), (1, -1, 0), (-1, 1, 0), (1, 0, 1), (-1, 0, -1), (1, 0, -1), (-1, 0, 1),
              (0, 1, 1), (0, -1, -1), (0, 1, -1), (0, -1, 1)]
OPPOSITE = [0, 2, 1, 4, 3, 6, 5, 8, 7, 10, 9, 12, 11, 14, 13, 16, 15, 18, 17]
LATTICE_WEIGHTS = [1.0 / 3.0] + [1.0 / 18.0] * 6 + [1.0 / 36.0] * 12
RELAX_TIME = 0.8
SPEED_SCALE = 0.05


def moments(populations):
    density = jnp.sum(populations, axis=0)
    components = []
    for column in range(3):
        summed = jnp.zeros_like(density)
        for member in range(19):
            factor = VELOCITIES[member][column]
            if factor != 0:
                summed = summed + factor * populations[member]
        components.append(summed / density)
    return density, jnp.stack(components)


def collide(populations, density, shifted, fluid_cells):
    squared = 1.5 * (shifted[0] * shifted[0] + shifted[1] * shifted[1] + shifted[2] * shifted[2])
    result = []
    for member in range(19):
        vector = VELOCITIES[member]
        projected = vector[0] * shifted[0] + vector[1] * shifted[1] + vector[2] * shifted[2]
        equilibrium = LATTICE_WEIGHTS[member] * density * (1.0 + 3.0 * projected + 4.5 * projected * projected - squared)
        relaxed = populations[member] + (equilibrium - populations[member]) / RELAX_TIME
        result.append(jnp.where(fluid_cells, relaxed, populations[OPPOSITE[member]]))
    return jnp.stack(result)


def reference(populations, solid_mask, whirl_offsets, marker_cells, marker_weights, pipe_velocity):
    fluid_cells = solid_mask == 0
    depth = jnp.arange(NZ, dtype=jnp.int32)[:, None, None, None]
    offsets = jnp.arange(4, dtype=jnp.int32)
    kernel = jnp.transpose(marker_weights[0], (1, 2, 0))[:, :, :, None] * jnp.transpose(marker_weights[1], (1, 2, 0))[:, :, None, :]
    force_markers = jnp.zeros(pipe_velocity.shape, jnp.float32)
    for iteration in range(STEPS):
        density, velocity = moments(populations)
        base_x = (NX // 2 + whirl_offsets[iteration, 0] + marker_cells[0] - 1).astype(jnp.int32)
        base_y = (NY // 2 + whirl_offsets[iteration, 1] + marker_cells[1] - 1).astype(jnp.int32)
        cells_x = base_x[:, :, None, None] + offsets[:, None]
        cells_y = base_y[:, :, None, None] + offsets[None, :]
        boxes = velocity[:, depth, cells_x, cells_y]
        sampled = jnp.sum(boxes * kernel[None], axis=(3, 4))
        force_markers = pipe_velocity - sampled
        body_force = jnp.zeros_like(velocity).at[:, depth, cells_x, cells_y].add(force_markers[:, :, :, None, None] * kernel[None])
        shifted = velocity + RELAX_TIME * body_force / density
        post = collide(populations, density, shifted, fluid_cells)
        populations = jnp.stack([jnp.roll(post[member], VELOCITIES[member], axis=(0, 1, 2)) for member in range(19)])
    density, velocity = moments(populations)
    velocity_field = jnp.where(fluid_cells, velocity / SPEED_SCALE, 0.0)
    return populations, velocity_field, force_markers / SPEED_SCALE
```

```python
import functools

import jax
import jax.numpy as jnp
from jax import lax
from jax.experimental import pallas as pl
from jax.experimental.pallas import tpu as pltpu
from jax.sharding import PartitionSpec as P

MESH = pl.DeviceIdType.MESH
STEPS = 3
RELAX_TIME = 0.8
SPEED_SCALE = 0.05

VELOCITIES = [
    (0, 0, 0),
    (1, 0, 0),
    (-1, 0, 0),
    (0, 1, 0),
    (0, -1, 0),
    (0, 0, 1),
    (0, 0, -1),
    (1, 1, 0),
    (-1, -1, 0),
    (1, -1, 0),
    (-1, 1, 0),
    (1, 0, 1),
    (-1, 0, -1),
    (1, 0, -1),
    (-1, 0, 1),
    (0, 1, 1),
    (0, -1, -1),
    (0, 1, -1),
    (0, -1, 1),
]
INDEX = {vector: member for member, vector in enumerate(VELOCITIES)}
INPLANE = [
    (0, 0, 0),
    (0, 0, 1),
    (0, 0, -1),
    (0, 1, 0),
    (0, 1, 1),
    (0, 1, -1),
    (0, -1, 0),
    (0, -1, 1),
    (0, -1, -1),
]
AXIAL = [
    [(1, 0, 0), (1, 0, 1), (1, 0, -1), (1, 1, 0), (1, -1, 0)],
    [(-1, 0, 0), (-1, 0, 1), (-1, 0, -1), (-1, 1, 0), (-1, -1, 0)],
]
EDGES = [
    (0, 0, 1),
    (0, 0, -1),
    (0, 1, 1),
    (0, 1, -1),
    (0, -1, 1),
    (0, -1, -1),
    (1, 0, 1),
    (1, 0, -1),
    (-1, 0, 1),
    (-1, 0, -1),
]
DIAGONAL = [(0, 1, 1), (0, 1, -1), (0, -1, 1), (0, -1, -1)]

BLOCKS = 8
OUTER_BLOCKS = 3
OUTER_ROWS = 24
CENTRE_ROWS = 40
N_AXIAL = 0
N_AXIAL_ROW = 4
N_ROW = 8
N_EDGE = 10
N_SAMPLE = 15
N_MESSAGES = 24


def tree_sum(values):
    while len(values) > 1:
        pairs = [values[i] + values[i + 1] for i in range(0, len(values) - 1, 2)]
        if len(values) % 2:
            pairs.append(values[-1])
        values = pairs
    return values[0]


def moments(f):
    density = tree_sum(f)
    inverse = 1.0 / density
    components = []
    for column in range(3):
        ahead = tree_sum([f[m] for m in range(19) if VELOCITIES[m][column] == 1])
        back = tree_sum([f[m] for m in range(19) if VELOCITIES[m][column] == -1])
        components.append((ahead - back) * inverse)
    return density, inverse, components


def dot(vector, u):
    total = None
    for c, x in zip(vector, u):
        if c == 0:
            continue
        if total is None:
            total = x if c == 1 else -x
        else:
            total = total + x if c == 1 else total - x
    return total


def collide(f, density, u, fluid):
    base = 1.0 - 1.5 * (u[0] * u[0] + u[1] * u[1] + u[2] * u[2])
    keep = 1.0 - 1.0 / RELAX_TIME
    scaled = density * (1.0 / RELAX_TIME)
    heavy = scaled * (1.0 / 18.0)
    light = scaled * (1.0 / 36.0)
    post = [None] * 19
    post[0] = jnp.where(fluid, scaled * (1.0 / 3.0) * base + keep * f[0], f[0])
    for m in range(1, 19, 2):
        weight = heavy if m < 7 else light
        projected = dot(VELOCITIES[m], u)
        even = weight * (base + 4.5 * (projected * projected))
        odd = (3.0 * weight) * projected
        post[m] = jnp.where(fluid, (even + odd) + keep * f[m], f[m + 1])
        post[m + 1] = jnp.where(fluid, (even - odd) + keep * f[m + 1], f[m])
    return post


def split(x):
    high = x.astype(jnp.bfloat16)
    low = (x - high.astype(jnp.float32)).astype(jnp.bfloat16)
    return high, low


def product(x, w_high, w_low, dims):
    high, low = split(x)
    one = functools.partial(
        lax.dot_general, dimension_numbers=(dims, ((), ())), preferred_element_type=jnp.float32
    )
    return one(high, w_high) + (one(low, w_high) + one(high, w_low))


def kernel(
    gz_size,
    pops,
    solid,
    whirl,
    cells,
    weights,
    target,
    out_pops,
    out_vel,
    out_force,
    pb,
    zs,
    zr,
    es,
    er,
    pp,
    st,
    mom,
    fb,
    mk_own,
    mk_all,
    mk,
    sp,
    wx,
    wy_high,
    wy_low,
    send_sem,
    recv_sem,
    mk_send,
    mk_recv,
):
    gz = lax.axis_index("gz")
    gx = lax.axis_index("gx")
    gy = lax.axis_index("gy")
    z_next, z_prev = lax.rem(gz + 1, gz_size), lax.rem(gz + gz_size - 1, gz_size)
    x_next, x_prev, x_far = lax.rem(gx + 1, 4), lax.rem(gx + 3, 4), lax.rem(gx + 2, 4)
    y_other = 1 - gy
    flip = gx // 2
    is_centre = lax.rem((gx + 1) // 2, 2)
    centre = is_centre == 1
    outer = is_centre == 0
    quarter = lax.rem(2 * gx + gy + 2, 4)
    own = 2 * gx + gy
    outer_start = pl.multiple_of(40 * flip, 8)
    centre_start = pl.multiple_of(24 * (1 - flip), 8)

    barrier = pltpu.get_barrier_semaphore()
    neighbours = [
        {"gz": gz, "gx": x_next, "gy": gy},
        {"gz": gz, "gx": x_prev, "gy": gy},
        {"gz": gz, "gx": x_far, "gy": gy},
        {"gz": gz, "gx": gx, "gy": y_other},
        {"gz": gz, "gx": x_next, "gy": y_other},
        {"gz": gz, "gx": x_prev, "gy": y_other},
        {"gz": gz, "gx": x_far, "gy": y_other},
    ]
    for z in (z_next, z_prev):
        neighbours += [
            {"gz": z, "gx": gx, "gy": gy},
            {"gz": z, "gx": x_next, "gy": gy},
            {"gz": z, "gx": x_prev, "gy": gy},
            {"gz": z, "gx": gx, "gy": y_other},
        ]
    for place in neighbours:
        pl.semaphore_signal(barrier, inc=1, device_id=place, device_id_type=MESH)

    lane = lax.broadcasted_iota(jnp.int32, (8, 128), 1)
    lane_block = lane // 16

    def block_of(b):
        return b + flip * (BLOCKS - 1 - 2 * b)

    def remote(src, dst, s, n, place, n_recv=None):
        return pltpu.make_async_remote_copy(
            src_ref=src,
            dst_ref=dst,
            send_sem=send_sem.at[s, n],
            recv_sem=recv_sem.at[s, n if n_recv is None else n_recv],
            device_id=place,
            device_id_type=MESH,
        )

    def axial(s, way, part):
        start, size = ((outer_start, OUTER_ROWS), (centre_start, CENTRE_ROWS))[part]
        return remote(
            zs.at[s, way, :, pl.ds(start, size), :],
            zr.at[s, way, :, pl.ds(pl.multiple_of(start + 8, 8), size), :],
            s,
            N_AXIAL + 2 * way + part,
            {"gz": (z_next, z_prev)[way], "gx": gx, "gy": gy},
        )

    def small(s):
        copies = []
        for way in range(2):
            z = (z_next, z_prev)[way]
            copies.append(
                remote(
                    zs.at[s, way, 3, pl.ds(56, 8), :],
                    zr.at[s, way, 3, pl.ds(0, 8), :],
                    s,
                    N_AXIAL_ROW + 2 * way,
                    {"gz": z, "gx": x_next, "gy": gy},
                )
            )
            copies.append(
                remote(
                    zs.at[s, way, 4, pl.ds(0, 8), :],
                    zr.at[s, way, 4, pl.ds(72, 8), :],
                    s,
                    N_AXIAL_ROW + 2 * way + 1,
                    {"gz": z, "gx": x_prev, "gy": gy},
                )
            )
        copies.append(
            remote(
                pb.at[s, pl.ds(3, 3), pl.ds(64, 8), :],
                pb.at[s, pl.ds(3, 3), pl.ds(0, 8), :],
                s,
                N_ROW,
                {"gz": gz, "gx": x_next, "gy": gy},
            )
        )
        copies.append(
            remote(
                pb.at[s, pl.ds(6, 3), pl.ds(8, 8), :],
                pb.at[s, pl.ds(6, 3), pl.ds(72, 8), :],
                s,
                N_ROW + 1,
                {"gz": gz, "gx": x_prev, "gy": gy},
            )
        )
        places = [
            {"gz": gz, "gx": gx, "gy": y_other},
            {"gz": gz, "gx": x_next, "gy": y_other},
            {"gz": gz, "gx": x_prev, "gy": y_other},
            {"gz": z_next, "gx": gx, "gy": y_other},
            {"gz": z_prev, "gx": gx, "gy": y_other},
        ]
        for k, place in enumerate(places):
            copies.append(remote(es.at[s], er.at[s, k], s, N_EDGE + k, place))
        return copies

    def sample_copies(s):
        pair = 3 - gx
        places = [(gx, y_other), (pair, gy), (pair, y_other)]
        if s == STEPS - 1:
            places += [(0, gy), (0, y_other), (3, gy), (3, y_other)]
        return [
            remote(
                sp.at[s, quarter],
                sp.at[s, quarter],
                s,
                N_SAMPLE + d,
                {"gz": gz, "gx": x, "gy": y},
                N_SAMPLE + quarter,
            )
            for d, (x, y) in enumerate(places)
        ]

    def sample_wait(s, q):
        remote(sp.at[s, q], sp.at[s, q], s, N_SAMPLE, neighbours[0], N_SAMPLE + q).wait_recv()

    def centre_place(t):
        return {"gz": gz, "gx": 1 + t // 2, "gy": t % 2}

    def marker_copy(t):
        return pltpu.make_async_remote_copy(
            src_ref=mk_all.at[own],
            dst_ref=mk_all.at[own],
            send_sem=mk_send.at[t],
            recv_sem=mk_recv.at[own],
            device_id=centre_place(t),
            device_id_type=MESH,
        )

    def marker_wait(j):
        pltpu.make_async_remote_copy(
            src_ref=mk_all.at[j],
            dst_ref=mk_all.at[j],
            send_sem=mk_send.at[0],
            recv_sem=mk_recv.at[j],
            device_id=neighbours[0],
            device_id_type=MESH,
        ).wait_recv()

    def not_self(t):
        return jnp.logical_or(gx != 1 + t // 2, gy != t % 2)

    def edge(value, packed, vector):
        j = EDGES.index(vector)
        if vector[2] == 1:
            there = packed if j == 0 else pltpu.roll(packed, 128 - j, 1)
            return jnp.where(lane == 0, there, value)
        return jnp.where(lane == 127, pltpu.roll(packed, 127 - j, 1), value)

    def gather(s, rb):
        row = pl.multiple_of(rb * 8, 8)
        if s == 0:
            return [pops[m, 0, pl.ds(row, 8), :] for m in range(19)]
        back = lax.rem(128 - 16 * rb, 128)
        packed = {
            0: pltpu.roll(er[s - 1, 0], back, 1),
            1: pltpu.roll(er[s - 1, 3], back, 1),
            -1: pltpu.roll(er[s - 1, 4], back, 1),
        }
        f = []
        for vector in VELOCITIES:
            rows = pl.ds(row + (8 - vector[1]), 8)
            if vector in DIAGONAL:
                f.append(pp[DIAGONAL.index(vector), rows, :])
                continue
            if vector[0] == 0:
                value = pb[s - 1, INPLANE.index(vector), rows, :]
            else:
                way = 0 if vector[0] == 1 else 1
                value = zr[s - 1, way, AXIAL[way].index(vector), rows, :]
            if vector[2] != 0:
                value = edge(value, packed[vector[0]], vector)
            f.append(value)
        return f

    def patch(s):
        def block(rb, carry):
            row = pl.multiple_of(rb * 8 + 8, 8)
            packed = pltpu.roll(er[s - 1, 0], lax.rem(128 - 16 * rb, 128), 1)
            for k, vector in enumerate(DIAGONAL):
                value = pb[s - 1, INPLANE.index(vector), pl.ds(row, 8), :]
                pp[k, pl.ds(row, 8), :] = edge(value, packed, vector)
            return carry

        lax.fori_loop(0, BLOCKS, block, 0)
        before = pltpu.roll(er[s - 1, 1], 16, 1)
        after = er[s - 1, 2]
        for k, vector in enumerate(DIAGONAL):
            packed, row = (before, 0) if vector[1] == 1 else (after, 72)
            value = pb[s - 1, INPLANE.index(vector), pl.ds(row, 8), :]
            pp[k, pl.ds(row, 8), :] = edge(value, packed, vector)

    def store_post(s, rb, post):
        row = pl.multiple_of(rb * 8, 8)
        for vector in VELOCITIES:
            value = post[INDEX[vector]]
            if vector[2] != 0:
                value = pltpu.roll(value, 1 if vector[2] == 1 else 127, 1)
            if vector[0] == 0:
                pb[s, INPLANE.index(vector), pl.ds(pl.multiple_of(row + 8, 8), 8), :] = value
            else:
                way = 0 if vector[0] == 1 else 1
                zs[s, way, AXIAL[way].index(vector), pl.ds(row, 8), :] = value
        packed = post[INDEX[EDGES[0]]]
        packed = pltpu.roll(packed, 1, 1)
        for j, vector in enumerate(EDGES):
            if j == 0:
                continue
            shift = j + 1 if vector[2] == 1 else j
            packed = jnp.where(lane == j, pltpu.roll(post[INDEX[vector]], shift, 1), packed)
        es[s] = jnp.where(lane_block == rb, pltpu.roll(packed, 16 * rb, 1), es[s])

    def fluid_of(rb):
        return solid[0, pl.ds(pl.multiple_of(rb * 8, 8), 8), :] == 0

    def whole_block(s):
        def block(b, carry):
            rb = block_of(b)
            f = gather(s, rb)
            density, _, u = moments(f)
            store_post(s, rb, collide(f, density, u, fluid_of(rb)))
            return carry

        return block

    def first_half(s):
        def block(b, carry):
            rb = block_of(b)
            row = pl.multiple_of(rb * 8, 8)
            f = gather(s, rb)
            density, inverse, u = moments(f)
            if s > 0:
                for m in range(19):
                    st[m, pl.ds(row, 8), :] = f[m]
            for c, value in enumerate([*u, density, inverse]):
                mom[c, pl.ds(row, 8), :] = value
            return carry

        return block

    def second_half(s):
        def block(b, carry):
            rb = block_of(b)
            row = pl.multiple_of(rb * 8, 8)
            if s == 0:
                f = [pops[m, 0, pl.ds(row, 8), :] for m in range(19)]
            else:
                f = [st[m, pl.ds(row, 8), :] for m in range(19)]
            density = mom[3, pl.ds(row, 8), :]
            scale = RELAX_TIME * mom[4, pl.ds(row, 8), :]
            near = pl.multiple_of(row - centre_start, 8)
            u = [mom[c, pl.ds(row, 8), :] + scale * fb[c, pl.ds(near, 8), :] for c in range(3)]
            store_post(s, rb, collide(f, density, u, fluid_of(rb)))
            return carry

        return block

    def marker_matrices(s):
        def matrix(size, first, base, row):
            place = lax.broadcasted_iota(jnp.int32, (size, 256), 0) + first
            distance = place.astype(jnp.float32) - base
            result = jnp.zeros((size, 256), jnp.float32)
            for a in range(4):
                result = jnp.where(distance == float(a), mk[row + a : row + a + 1, :], result)
            return result

        base_x = mk[0:1, :] + (127 + whirl[s, 0]).astype(jnp.float32)
        base_y = mk[1:2, :] + (127 + whirl[s, 1]).astype(jnp.float32)
        wx[...] = matrix(CENTRE_ROWS, 64 * gx + centre_start, base_x, 2)
        high, low = split(matrix(128, 128 * gy, base_y, 6))
        wy_high[...] = high
        wy_low[...] = low

    def sample(s):
        u = mom[0:3, pl.ds(centre_start, CENTRE_ROWS), :].reshape(3 * CENTRE_ROWS, 128)
        along = product(u, wy_high[...], wy_low[...], ((1,), (0,)))
        spread = wx[...]
        rows = [
            jnp.sum(along[c * CENTRE_ROWS : (c + 1) * CENTRE_ROWS] * spread, axis=0, keepdims=True)
            for c in range(3)
        ]
        sp[s, quarter] = jnp.concatenate(rows + [jnp.zeros((5, 256), jnp.float32)], axis=0)

    def sampled(s):
        return (sp[s, 0] + sp[s, 1]) + (sp[s, 2] + sp[s, 3])

    def force(s):
        push = mk[10:13, :] - sampled(s)[0:3, :]
        spread = wx[...]
        weighted = jnp.concatenate([spread * push[c : c + 1, :] for c in range(3)], axis=0)
        body = product(weighted, wy_high[...], wy_low[...], ((1,), (1,)))
        fb[...] = body.reshape(3, CENTRE_ROWS, 128)

    mk_own[...] = jnp.zeros((16, 128), jnp.float32)
    mk_own[0:2, 0:32] = cells[:, 0, :].astype(jnp.float32)
    mk_own[2:6, 0:32] = weights[0, :, 0, :]
    mk_own[6:10, 0:32] = weights[1, :, 0, :]
    mk_own[10:13, 0:32] = target[:, 0, :]
    mk_all[own] = pltpu.roll(mk_own[...], 32 * lax.rem(own, 4), 1)

    pl.semaphore_wait(barrier, len(neighbours))

    for t in range(4):

        @pl.when(not_self(t))
        def _(t=t):
            marker_copy(t).start()

    for s in range(STEPS):
        last = s == STEPS - 1
        if s > 0:
            for copy in [axial(s - 1, way, part) for way in range(2) for part in range(2)] + small(s - 1):
                copy.wait_recv()
            patch(s)

        @pl.when(centre)
        def _(s=s):
            lax.fori_loop(OUTER_BLOCKS, BLOCKS, first_half(s), 0)
            if s == 0:
                for d in range(1, 8):
                    marker_wait(lax.rem(own + d, 8))
                mk[:, 0:128] = (mk_all[0] + mk_all[1]) + (mk_all[2] + mk_all[3])
                mk[:, 128:256] = (mk_all[4] + mk_all[5]) + (mk_all[6] + mk_all[7])
                marker_matrices(s)
            sample(s)
            for copy in sample_copies(s):
                copy.start()

        lax.fori_loop(0, OUTER_BLOCKS, whole_block(s), 0)
        for way in range(2):
            axial(s, way, 0).start()

        @pl.when(outer)
        def _(s=s):
            lax.fori_loop(OUTER_BLOCKS, BLOCKS, whole_block(s), 0)

        @pl.when(centre)
        def _(s=s):
            for d in range(1, 4):
                sample_wait(s, lax.rem(quarter + d, 4))
            force(s)
            lax.fori_loop(OUTER_BLOCKS, BLOCKS, second_half(s), 0)

        for way in range(2):
            axial(s, way, 1).start()
        for copy in small(s):
            copy.start()

        if not last:

            @pl.when(centre)
            def _(s=s):
                marker_matrices(s + 1)

    for copy in [axial(STEPS - 1, way, part) for way in range(2) for part in range(2)] + small(STEPS - 1):
        copy.wait_recv()
    patch(STEPS)

    def final_block(rb, carry):
        rows = pl.ds(pl.multiple_of(rb * 8, 8), 8)
        f = gather(STEPS, rb)
        for m in range(19):
            out_pops[m, 0, rows, :] = f[m]
        _, _, u = moments(f)
        fluid = fluid_of(rb)
        for c in range(3):
            out_vel[c, 0, rows, :] = jnp.where(fluid, u[c] * (1.0 / SPEED_SCALE), 0.0)
        return carry

    lax.fori_loop(0, BLOCKS, final_block, 0)

    @pl.when(outer)
    def _():
        for q in range(4):
            sample_wait(STEPS - 1, q)

    total = sampled(STEPS - 1)
    half = jnp.where(own // 4 == 0, total[:, 0:128], total[:, 128:256])
    half = pltpu.roll(half, lax.rem(128 - 32 * lax.rem(own, 4), 128), 1)
    out_force[:, 0, :] = (target[:, 0, :] - half[0:3, 0:32]) * (1.0 / SPEED_SCALE)

    for t in range(4):

        @pl.when(not_self(t))
        def _(t=t):
            marker_copy(t).wait_send()

    for s in range(STEPS):
        for copy in [axial(s, way, part) for way in range(2) for part in range(2)] + small(s):
            copy.wait_send()

    @pl.when(centre)
    def _():
        for s in range(STEPS):
            for copy in sample_copies(s):
                copy.wait_send()


def body(populations, solid_mask, whirl_offsets, marker_cells, marker_weights, pipe_velocity):
    f32 = jnp.float32
    vmem = pl.BlockSpec(memory_space=pltpu.VMEM)
    return pl.pallas_call(
        functools.partial(kernel, lax.axis_size("gz")),
        out_shape=(
            jax.ShapeDtypeStruct(populations.shape, f32),
            jax.ShapeDtypeStruct((3,) + solid_mask.shape, f32),
            jax.ShapeDtypeStruct(pipe_velocity.shape, f32),
        ),
        in_specs=[vmem, vmem, pl.BlockSpec(memory_space=pltpu.SMEM), vmem, vmem, vmem],
        out_specs=(vmem, vmem, vmem),
        scratch_shapes=[
            pltpu.VMEM((STEPS, 9, 80, 128), f32),
            pltpu.VMEM((STEPS, 2, 5, 64, 128), f32),
            pltpu.VMEM((STEPS, 2, 5, 80, 128), f32),
            pltpu.VMEM((STEPS, 8, 128), f32),
            pltpu.VMEM((STEPS, 5, 8, 128), f32),
            pltpu.VMEM((4, 80, 128), f32),
            pltpu.VMEM((19, 64, 128), f32),
            pltpu.VMEM((5, 64, 128), f32),
            pltpu.VMEM((3, CENTRE_ROWS, 128), f32),
            pltpu.VMEM((16, 128), f32),
            pltpu.VMEM((8, 16, 128), f32),
            pltpu.VMEM((16, 256), f32),
            pltpu.VMEM((STEPS, 4, 8, 256), f32),
            pltpu.VMEM((CENTRE_ROWS, 256), f32),
            pltpu.VMEM((128, 256), jnp.bfloat16),
            pltpu.VMEM((128, 256), jnp.bfloat16),
            pltpu.SemaphoreType.DMA((STEPS, N_MESSAGES)),
            pltpu.SemaphoreType.DMA((STEPS, N_MESSAGES)),
            pltpu.SemaphoreType.DMA((4,)),
            pltpu.SemaphoreType.DMA((8,)),
        ],
        compiler_params=pltpu.CompilerParams(
            collective_id=0, has_side_effects=True, vmem_limit_bytes=24 * 1024 * 1024
        ),
        cost_estimate=pl.CostEstimate(flops=40_000_000, bytes_accessed=2_000_000, transcendentals=0),
    )(populations, solid_mask, whirl_offsets, marker_cells, marker_weights, pipe_velocity)


def solution(mesh):
    in_specs = (
        P(None, "gz", "gx", "gy"),
        P("gz", "gx", "gy"),
        P(),
        P(None, "gz", ("gx", "gy")),
        P(None, None, "gz", ("gx", "gy")),
        P(None, "gz", ("gx", "gy")),
    )
    out_specs = (P(None, "gz", "gx", "gy"), P(None, "gz", "gx", "gy"), P(None, "gz", ("gx", "gy")))
    return jax.shard_map(body, mesh=mesh, in_specs=in_specs, out_specs=out_specs, check_vma=False)
```

```python
import functools

import jax
import jax.numpy as jnp
from jax import lax
from jax.experimental import pallas as pl
from jax.experimental.pallas import tpu as pltpu
from jax.sharding import PartitionSpec as P

MESH = pl.DeviceIdType.MESH
STEPS = 3
RELAX_TIME = 0.8
SPEED_SCALE = 0.05

VELOCITIES = [
    (0, 0, 0),
    (1, 0, 0),
    (-1, 0, 0),
    (0, 1, 0),
    (0, -1, 0),
    (0, 0, 1),
    (0, 0, -1),
    (1, 1, 0),
    (-1, -1, 0),
    (1, -1, 0),
    (-1, 1, 0),
    (1, 0, 1),
    (-1, 0, -1),
    (1, 0, -1),
    (-1, 0, 1),
    (0, 1, 1),
    (0, -1, -1),
    (0, 1, -1),
    (0, -1, 1),
]
INDEX = {vector: member for member, vector in enumerate(VELOCITIES)}
INPLANE = [
    (0, 0, 0),
    (0, 0, 1),
    (0, 0, -1),
    (0, 1, 0),
    (0, 1, 1),
    (0, 1, -1),
    (0, -1, 0),
    (0, -1, 1),
    (0, -1, -1),
]
AXIAL = [
    [(1, 0, 0), (1, 0, 1), (1, 0, -1), (1, 1, 0), (1, -1, 0)],
    [(-1, 0, 0), (-1, 0, 1), (-1, 0, -1), (-1, 1, 0), (-1, -1, 0)],
]
EDGES = [
    (0, 0, 1),
    (0, 0, -1),
    (0, 1, 1),
    (0, 1, -1),
    (0, -1, 1),
    (0, -1, -1),
    (1, 0, 1),
    (1, 0, -1),
    (-1, 0, 1),
    (-1, 0, -1),
]
DIAGONAL = [(0, 1, 1), (0, 1, -1), (0, -1, 1), (0, -1, -1)]

SIZE = 16
BLOCKS = 4
OUTER_BLOCKS = 1
OUTER_ROWS = SIZE * OUTER_BLOCKS
CENTRE_ROWS = SIZE * (BLOCKS - OUTER_BLOCKS)
SPAN = 128 // BLOCKS
N_AXIAL = 0
N_AXIAL_ROW = 4
N_ROW = 8
N_EDGE = 10
N_SAMPLE = 15
N_MESSAGES = 24


def tree_sum(values):
    while len(values) > 1:
        pairs = [values[i] + values[i + 1] for i in range(0, len(values) - 1, 2)]
        if len(values) % 2:
            pairs.append(values[-1])
        values = pairs
    return values[0]


def moments(f):
    density = tree_sum(f)
    inverse = 1.0 / density
    components = []
    for column in range(3):
        ahead = tree_sum([f[m] for m in range(19) if VELOCITIES[m][column] == 1])
        back = tree_sum([f[m] for m in range(19) if VELOCITIES[m][column] == -1])
        components.append((ahead - back) * inverse)
    return density, inverse, components


def dot(vector, u):
    total = None
    for c, x in zip(vector, u):
        if c == 0:
            continue
        if total is None:
            total = x if c == 1 else -x
        else:
            total = total + x if c == 1 else total - x
    return total


def collide(f, density, u, fluid):
    base = 1.0 - 1.5 * (u[0] * u[0] + u[1] * u[1] + u[2] * u[2])
    keep = 1.0 - 1.0 / RELAX_TIME
    scaled = density * (1.0 / RELAX_TIME)
    heavy = scaled * (1.0 / 18.0)
    light = scaled * (1.0 / 36.0)
    post = [None] * 19
    post[0] = jnp.where(fluid, scaled * (1.0 / 3.0) * base + keep * f[0], f[0])
    for m in range(1, 19, 2):
        weight = heavy if m < 7 else light
        projected = dot(VELOCITIES[m], u)
        even = weight * (base + 4.5 * (projected * projected))
        odd = (3.0 * weight) * projected
        post[m] = jnp.where(fluid, (even + odd) + keep * f[m], f[m + 1])
        post[m + 1] = jnp.where(fluid, (even - odd) + keep * f[m + 1], f[m])
    return post


def split(x):
    high = x.astype(jnp.bfloat16)
    low = (x - high.astype(jnp.float32)).astype(jnp.bfloat16)
    return high, low


def product(x, w_high, w_low, dims):
    high, low = split(x)
    one = functools.partial(
        lax.dot_general, dimension_numbers=(dims, ((), ())), preferred_element_type=jnp.float32
    )
    return one(high, w_high) + (one(low, w_high) + one(high, w_low))


def edge(value, packed, vector):
    j = EDGES.index(vector)
    lane = lax.broadcasted_iota(jnp.int32, value.shape, 1)
    if vector[2] == 1:
        there = packed if j == 0 else pltpu.roll(packed, 128 - j, 1)
        return jnp.where(lane == 0, there, value)
    return jnp.where(lane == 127, pltpu.roll(packed, 127 - j, 1), value)


def unpacked(packed, rb):
    return pltpu.roll(packed, lax.rem(128 - SPAN * rb, 128), 1)


def patch(pb, er, pp):
    def block(rb, carry):
        row = pl.multiple_of(rb * SIZE + 8, 8)
        packed = unpacked(er[0], rb)
        for k, vector in enumerate(DIAGONAL):
            value = pb[INPLANE.index(vector), pl.ds(row, SIZE), :]
            pp[k, pl.ds(row, SIZE), :] = edge(value, packed, vector)
        return carry

    lax.fori_loop(0, BLOCKS, block, 0)
    before = pltpu.roll(er[1, SIZE - 8 :, :], SPAN, 1)
    after = er[2, 0:8, :]
    for k, vector in enumerate(DIAGONAL):
        packed, row = (before, 0) if vector[1] == 1 else (after, 72)
        value = pb[INPLANE.index(vector), pl.ds(row, 8), :]
        pp[k, pl.ds(row, 8), :] = edge(value, packed, vector)


def streamed(pb, zr, er, pp, rb):
    row = pl.multiple_of(rb * SIZE, 8)
    packed = {0: unpacked(er[0], rb), 1: unpacked(er[3], rb), -1: unpacked(er[4], rb)}
    f = []
    for vector in VELOCITIES:
        rows = pl.ds(row + (8 - vector[1]), SIZE)
        if vector in DIAGONAL:
            f.append(pp[DIAGONAL.index(vector), rows, :])
            continue
        if vector[0] == 0:
            value = pb[INPLANE.index(vector), rows, :]
        else:
            way = 0 if vector[0] == 1 else 1
            value = zr[way, AXIAL[way].index(vector), rows, :]
        if vector[2] != 0:
            value = edge(value, packed[vector[0]], vector)
        f.append(value)
    return f


def kernel(
    gz_size,
    pops_in,
    solid_in,
    whirl_in,
    cells_in,
    weights_in,
    target_in,
    pb_last,
    zr_last,
    er_last,
    force_last,
    pb_early,
    zs,
    zr_early,
    es,
    er_early,
    pp,
    st,
    mom,
    fb,
    mk_own,
    mk_all,
    mk,
    sp,
    wx,
    wy_high,
    wy_low,
    send_sem,
    recv_sem,
    mk_send,
    mk_recv,
    pops,
    solid,
    whirl,
    cells,
    weights,
    target,
    load_sem,
):
    loads = [
        pltpu.make_async_copy(src, dst, load_sem.at[k])
        for k, (src, dst) in enumerate(
            [
                (cells_in, cells),
                (weights_in, weights),
                (target_in, target),
                (whirl_in, whirl),
                (pops_in, pops),
                (solid_in, solid),
            ]
        )
    ]
    for load in loads:
        load.start()
    pb = [pb_early.at[s] for s in range(STEPS - 1)] + [pb_last]
    zr = [zr_early.at[s] for s in range(STEPS - 1)] + [zr_last]
    er = [er_early.at[s] for s in range(STEPS - 1)] + [er_last]
    gz = lax.axis_index("gz")
    gx = lax.axis_index("gx")
    gy = lax.axis_index("gy")
    z_next, z_prev = lax.rem(gz + 1, gz_size), lax.rem(gz + gz_size - 1, gz_size)
    x_next, x_prev, x_far = lax.rem(gx + 1, 4), lax.rem(gx + 3, 4), lax.rem(gx + 2, 4)
    y_other = 1 - gy
    flip = gx // 2
    is_centre = lax.rem((gx + 1) // 2, 2)
    centre = is_centre == 1
    outer = is_centre == 0
    quarter = lax.rem(2 * gx + gy + 2, 4)
    own = 2 * gx + gy
    outer_start = pl.multiple_of(CENTRE_ROWS * flip, 8)
    centre_start = pl.multiple_of(OUTER_ROWS * (1 - flip), 8)

    barrier = pltpu.get_barrier_semaphore()
    neighbours = [
        {"gz": gz, "gx": x_next, "gy": gy},
        {"gz": gz, "gx": x_prev, "gy": gy},
        {"gz": gz, "gx": x_far, "gy": gy},
        {"gz": gz, "gx": gx, "gy": y_other},
        {"gz": gz, "gx": x_next, "gy": y_other},
        {"gz": gz, "gx": x_prev, "gy": y_other},
        {"gz": gz, "gx": x_far, "gy": y_other},
    ]
    for z in (z_next, z_prev):
        neighbours += [
            {"gz": z, "gx": gx, "gy": gy},
            {"gz": z, "gx": x_next, "gy": gy},
            {"gz": z, "gx": x_prev, "gy": gy},
            {"gz": z, "gx": gx, "gy": y_other},
        ]
    for place in neighbours:
        pl.semaphore_signal(barrier, inc=1, device_id=place, device_id_type=MESH)

    lanes = lax.broadcasted_iota(jnp.int32, (SIZE, 128), 1)
    lane_block = lanes // SPAN

    def block_of(b):
        return b + flip * (BLOCKS - 1 - 2 * b)

    def remote(src, dst, s, n, place, n_recv=None):
        return pltpu.make_async_remote_copy(
            src_ref=src,
            dst_ref=dst,
            send_sem=send_sem.at[s, n],
            recv_sem=recv_sem.at[s, n if n_recv is None else n_recv],
            device_id=place,
            device_id_type=MESH,
        )

    def axial(s, way, part):
        start, size = ((outer_start, OUTER_ROWS), (centre_start, CENTRE_ROWS))[part]
        return remote(
            zs.at[s, way, :, pl.ds(start, size), :],
            zr[s].at[way, :, pl.ds(pl.multiple_of(start + 8, 8), size), :],
            s,
            N_AXIAL + 2 * way + part,
            {"gz": (z_next, z_prev)[way], "gx": gx, "gy": gy},
        )

    def small(s):
        copies = []
        for way in range(2):
            z = (z_next, z_prev)[way]
            copies.append(
                remote(
                    zs.at[s, way, 3, pl.ds(56, 8), :],
                    zr[s].at[way, 3, pl.ds(0, 8), :],
                    s,
                    N_AXIAL_ROW + 2 * way,
                    {"gz": z, "gx": x_next, "gy": gy},
                )
            )
            copies.append(
                remote(
                    zs.at[s, way, 4, pl.ds(0, 8), :],
                    zr[s].at[way, 4, pl.ds(72, 8), :],
                    s,
                    N_AXIAL_ROW + 2 * way + 1,
                    {"gz": z, "gx": x_prev, "gy": gy},
                )
            )
        copies.append(
            remote(
                pb[s].at[pl.ds(3, 3), pl.ds(64, 8), :],
                pb[s].at[pl.ds(3, 3), pl.ds(0, 8), :],
                s,
                N_ROW,
                {"gz": gz, "gx": x_next, "gy": gy},
            )
        )
        copies.append(
            remote(
                pb[s].at[pl.ds(6, 3), pl.ds(8, 8), :],
                pb[s].at[pl.ds(6, 3), pl.ds(72, 8), :],
                s,
                N_ROW + 1,
                {"gz": gz, "gx": x_prev, "gy": gy},
            )
        )
        places = [
            {"gz": gz, "gx": gx, "gy": y_other},
            {"gz": gz, "gx": x_next, "gy": y_other},
            {"gz": gz, "gx": x_prev, "gy": y_other},
            {"gz": z_next, "gx": gx, "gy": y_other},
            {"gz": z_prev, "gx": gx, "gy": y_other},
        ]
        for k, place in enumerate(places):
            copies.append(remote(es.at[s], er[s].at[k], s, N_EDGE + k, place))
        return copies

    def sample_copies(s):
        pair = 3 - gx
        places = [(gx, y_other), (pair, gy), (pair, y_other)]
        if s == STEPS - 1:
            places += [(0, gy), (0, y_other), (3, gy), (3, y_other)]
        return [
            remote(
                sp.at[s, quarter],
                sp.at[s, quarter],
                s,
                N_SAMPLE + d,
                {"gz": gz, "gx": x, "gy": y},
                N_SAMPLE + quarter,
            )
            for d, (x, y) in enumerate(places)
        ]

    def sample_wait(s, q):
        remote(sp.at[s, q], sp.at[s, q], s, N_SAMPLE, neighbours[0], N_SAMPLE + q).wait_recv()

    def centre_place(t):
        return {"gz": gz, "gx": 1 + t // 2, "gy": t % 2}

    def marker_copy(t):
        return pltpu.make_async_remote_copy(
            src_ref=mk_all.at[own],
            dst_ref=mk_all.at[own],
            send_sem=mk_send.at[t],
            recv_sem=mk_recv.at[own],
            device_id=centre_place(t),
            device_id_type=MESH,
        )

    def marker_wait(j):
        pltpu.make_async_remote_copy(
            src_ref=mk_all.at[j],
            dst_ref=mk_all.at[j],
            send_sem=mk_send.at[0],
            recv_sem=mk_recv.at[j],
            device_id=neighbours[0],
            device_id_type=MESH,
        ).wait_recv()

    def not_self(t):
        return jnp.logical_or(gx != 1 + t // 2, gy != t % 2)

    def gather(s, rb):
        if s == 0:
            row = pl.multiple_of(rb * SIZE, 8)
            return [pops[m, 0, pl.ds(row, SIZE), :] for m in range(19)]
        return streamed(pb[s - 1], zr[s - 1], er[s - 1], pp, rb)

    def store_post(s, rb, post):
        row = pl.multiple_of(rb * SIZE, 8)
        for vector in VELOCITIES:
            value = post[INDEX[vector]]
            if vector[2] != 0:
                value = pltpu.roll(value, 1 if vector[2] == 1 else 127, 1)
            if vector[0] == 0:
                pb[s][INPLANE.index(vector), pl.ds(pl.multiple_of(row + 8, 8), SIZE), :] = value
            else:
                way = 0 if vector[0] == 1 else 1
                zs[s, way, AXIAL[way].index(vector), pl.ds(row, SIZE), :] = value
        packed = post[INDEX[EDGES[0]]]
        packed = pltpu.roll(packed, 1, 1)
        for j, vector in enumerate(EDGES):
            if j == 0:
                continue
            shift = j + 1 if vector[2] == 1 else j
            packed = jnp.where(lanes == j, pltpu.roll(post[INDEX[vector]], shift, 1), packed)
        es[s] = jnp.where(lane_block == rb, pltpu.roll(packed, SPAN * rb, 1), es[s])

    def fluid_of(rb):
        return solid[0, pl.ds(pl.multiple_of(rb * SIZE, 8), SIZE), :] == 0

    def whole_block(s):
        def block(b, carry):
            rb = block_of(b)
            f = gather(s, rb)
            density, _, u = moments(f)
            store_post(s, rb, collide(f, density, u, fluid_of(rb)))
            return carry

        return block

    def first_half(s):
        def block(b, carry):
            rb = block_of(b)
            row = pl.multiple_of(rb * SIZE, 8)
            f = gather(s, rb)
            density, inverse, u = moments(f)
            if s > 0:
                for m in range(19):
                    st[m, pl.ds(row, SIZE), :] = f[m]
            for c, value in enumerate([*u, density, inverse]):
                mom[c, pl.ds(row, SIZE), :] = value
            return carry

        return block

    def second_half(s):
        def block(b, carry):
            rb = block_of(b)
            row = pl.multiple_of(rb * SIZE, 8)
            if s == 0:
                f = [pops[m, 0, pl.ds(row, SIZE), :] for m in range(19)]
            else:
                f = [st[m, pl.ds(row, SIZE), :] for m in range(19)]
            density = mom[3, pl.ds(row, SIZE), :]
            scale = RELAX_TIME * mom[4, pl.ds(row, SIZE), :]
            near = pl.multiple_of(row - centre_start, 8)
            u = [mom[c, pl.ds(row, SIZE), :] + scale * fb[c, pl.ds(near, SIZE), :] for c in range(3)]
            store_post(s, rb, collide(f, density, u, fluid_of(rb)))
            return carry

        return block

    def marker_matrices(s):
        def matrix(size, first, base, row):
            place = lax.broadcasted_iota(jnp.int32, (size, 256), 0) + first
            distance = place.astype(jnp.float32) - base
            result = jnp.zeros((size, 256), jnp.float32)
            for a in range(4):
                result = jnp.where(distance == float(a), mk[row + a : row + a + 1, :], result)
            return result

        base_x = mk[0:1, :] + (127 + whirl[0, s]).astype(jnp.float32)
        base_y = mk[1:2, :] + (127 + whirl[1, s]).astype(jnp.float32)
        wx[...] = matrix(CENTRE_ROWS, 64 * gx + centre_start, base_x, 2)
        high, low = split(matrix(128, 128 * gy, base_y, 6))
        wy_high[...] = high
        wy_low[...] = low

    def sample(s):
        u = mom[0:3, pl.ds(centre_start, CENTRE_ROWS), :].reshape(3 * CENTRE_ROWS, 128)
        along = product(u, wy_high[...], wy_low[...], ((1,), (0,)))
        spread = wx[...]
        rows = [
            jnp.sum(along[c * CENTRE_ROWS : (c + 1) * CENTRE_ROWS] * spread, axis=0, keepdims=True)
            for c in range(3)
        ]
        sp[s, quarter] = jnp.concatenate(rows + [jnp.zeros((5, 256), jnp.float32)], axis=0)

    def sampled(s):
        return (sp[s, 0] + sp[s, 1]) + (sp[s, 2] + sp[s, 3])

    def force(s):
        push = mk[10:13, :] - sampled(s)[0:3, :]
        spread = wx[...]
        weighted = jnp.concatenate([spread * push[c : c + 1, :] for c in range(3)], axis=0)
        body = product(weighted, wy_high[...], wy_low[...], ((1,), (1,)))
        fb[...] = body.reshape(3, CENTRE_ROWS, 128)

    for load in loads[:4]:
        load.wait()
    mk_own[...] = jnp.zeros((16, 128), jnp.float32)
    mk_own[0:2, 0:32] = cells[:, 0, :].astype(jnp.float32)
    mk_own[2:6, 0:32] = weights[0, :, 0, :]
    mk_own[6:10, 0:32] = weights[1, :, 0, :]
    mk_own[10:13, 0:32] = target[:, 0, :]
    mk_all[own] = pltpu.roll(mk_own[...], 32 * lax.rem(own, 4), 1)

    pl.semaphore_wait(barrier, len(neighbours))

    for t in range(4):

        @pl.when(not_self(t))
        def _(t=t):
            marker_copy(t).start()

    for load in loads[4:]:
        load.wait()

    for s in range(STEPS):
        last = s == STEPS - 1
        if s > 0:
            for copy in [axial(s - 1, way, part) for way in range(2) for part in range(2)] + small(s - 1):
                copy.wait_recv()
            patch(pb[s - 1], er[s - 1], pp)

        @pl.when(centre)
        def _(s=s):
            lax.fori_loop(OUTER_BLOCKS, BLOCKS, first_half(s), 0)
            if s == 0:
                for d in range(1, 8):
                    marker_wait(lax.rem(own + d, 8))
                mk[:, 0:128] = (mk_all[0] + mk_all[1]) + (mk_all[2] + mk_all[3])
                mk[:, 128:256] = (mk_all[4] + mk_all[5]) + (mk_all[6] + mk_all[7])
                marker_matrices(s)
            sample(s)
            for copy in sample_copies(s):
                copy.start()

        lax.fori_loop(0, OUTER_BLOCKS, whole_block(s), 0)
        for way in range(2):
            axial(s, way, 0).start()

        @pl.when(outer)
        def _(s=s):
            lax.fori_loop(OUTER_BLOCKS, BLOCKS, whole_block(s), 0)

        @pl.when(centre)
        def _(s=s):
            for d in range(1, 4):
                sample_wait(s, lax.rem(quarter + d, 4))
            force(s)
            lax.fori_loop(OUTER_BLOCKS, BLOCKS, second_half(s), 0)

        for copy in small(s)[::-1]:
            copy.start()
        for way in range(2):
            axial(s, way, 1).start()

        if not last:

            @pl.when(centre)
            def _(s=s):
                marker_matrices(s + 1)

    for copy in [axial(STEPS - 1, way, part) for way in range(2) for part in range(2)] + small(STEPS - 1):
        copy.wait_recv()

    @pl.when(outer)
    def _():
        for q in range(4):
            sample_wait(STEPS - 1, q)

    total = sampled(STEPS - 1)
    half = jnp.where(own // 4 == 0, total[:, 0:128], total[:, 128:256])
    half = pltpu.roll(half, lax.rem(128 - 32 * lax.rem(own, 4), 128), 1)
    force_last[:, 0, :] = (target[:, 0, :] - half[0:3, 0:32]) * (1.0 / SPEED_SCALE)

    for t in range(4):

        @pl.when(not_self(t))
        def _(t=t):
            marker_copy(t).wait_send()

    for s in range(STEPS):
        for copy in [axial(s, way, part) for way in range(2) for part in range(2)] + small(s):
            copy.wait_send()

    @pl.when(centre)
    def _():
        for s in range(STEPS):
            for copy in sample_copies(s):
                copy.wait_send()


def finish(pb, zr, er, force, solid, res_pops, res_vel, res_force, pp, out_pops, out_vel, sem):
    patch(pb, er, pp)
    copies = []
    for rb in range(BLOCKS):
        rows = pl.ds(rb * SIZE, SIZE)
        f = streamed(pb, zr, er, pp, rb)
        for m in range(19):
            out_pops[m, 0, rows, :] = f[m]
        _, _, u = moments(f)
        fluid = solid[0, rows, :] == 0
        for c in range(3):
            out_vel[c, 0, rows, :] = jnp.where(fluid, u[c] * (1.0 / SPEED_SCALE), 0.0)
        for k, (src, dst) in enumerate([(out_pops, res_pops), (out_vel, res_vel)]):
            copy = pltpu.make_async_copy(
                src.at[:, :, rows, :], dst.at[:, :, rows, :], sem.at[2 * rb + k]
            )
            copy.start()
            copies.append(copy)
    copy = pltpu.make_async_copy(force, res_force, sem.at[2 * BLOCKS])
    copy.start()
    copies.append(copy)
    for copy in copies:
        copy.wait()


def body(populations, solid_mask, whirl_offsets, marker_cells, marker_weights, pipe_velocity):
    f32 = jnp.float32
    vmem = pl.BlockSpec(memory_space=pltpu.VMEM)
    hbm = pl.BlockSpec(memory_space=pltpu.HBM)
    pb, zr, er = (9, 80, 128), (2, 5, 80, 128), (5, SIZE, 128)
    arrived = pl.pallas_call(
        functools.partial(kernel, lax.axis_size("gz")),
        out_shape=[pltpu.VMEM(shape, f32) for shape in (pb, zr, er, pipe_velocity.shape)],
        in_specs=[hbm] * 6,
        out_specs=[vmem] * 4,
        scratch_shapes=[
            pltpu.VMEM((STEPS - 1,) + pb, f32),
            pltpu.VMEM((STEPS, 2, 5, 64, 128), f32),
            pltpu.VMEM((STEPS - 1,) + zr, f32),
            pltpu.VMEM((STEPS, SIZE, 128), f32),
            pltpu.VMEM((STEPS - 1,) + er, f32),
            pltpu.VMEM((4, 80, 128), f32),
            pltpu.VMEM((19, 64, 128), f32),
            pltpu.VMEM((5, 64, 128), f32),
            pltpu.VMEM((3, CENTRE_ROWS, 128), f32),
            pltpu.VMEM((16, 128), f32),
            pltpu.VMEM((8, 16, 128), f32),
            pltpu.VMEM((16, 256), f32),
            pltpu.VMEM((STEPS, 4, 8, 256), f32),
            pltpu.VMEM((CENTRE_ROWS, 256), f32),
            pltpu.VMEM((128, 256), jnp.bfloat16),
            pltpu.VMEM((128, 256), jnp.bfloat16),
            pltpu.SemaphoreType.DMA((STEPS, N_MESSAGES)),
            pltpu.SemaphoreType.DMA((STEPS, N_MESSAGES)),
            pltpu.SemaphoreType.DMA((4,)),
            pltpu.SemaphoreType.DMA((8,)),
            pltpu.VMEM(populations.shape, f32),
            pltpu.VMEM(solid_mask.shape, jnp.int32),
            pltpu.SMEM(whirl_offsets.shape[::-1], jnp.int32),
            pltpu.VMEM(marker_cells.shape, jnp.int32),
            pltpu.VMEM(marker_weights.shape, f32),
            pltpu.VMEM(pipe_velocity.shape, f32),
            pltpu.SemaphoreType.DMA((6,)),
        ],
        compiler_params=pltpu.CompilerParams(
            collective_id=0, has_side_effects=True, vmem_limit_bytes=60 * 1024 * 1024
        ),
        cost_estimate=pl.CostEstimate(flops=40_000_000, bytes_accessed=2_000_000, transcendentals=0),
    )(populations, solid_mask, whirl_offsets.T, marker_cells, marker_weights, pipe_velocity)
    shapes = (populations.shape, (3,) + solid_mask.shape, pipe_velocity.shape)
    return pl.pallas_call(
        finish,
        out_shape=[jax.ShapeDtypeStruct(shape, f32) for shape in shapes],
        in_specs=[vmem] * 5,
        out_specs=[hbm] * 3,
        scratch_shapes=[pltpu.VMEM((4, 80, 128), f32)]
        + [pltpu.VMEM(shape, f32) for shape in shapes[:2]]
        + [pltpu.SemaphoreType.DMA((2 * BLOCKS + 1,))],
        compiler_params=pltpu.CompilerParams(vmem_limit_bytes=24 * 1024 * 1024),
        cost_estimate=pl.CostEstimate(flops=2_000_000, bytes_accessed=2_000_000, transcendentals=0),
    )(*arrived, solid_mask)


def solution(mesh):
    in_specs = (
        P(None, "gz", "gx", "gy"),
        P("gz", "gx", "gy"),
        P(),
        P(None, "gz", ("gx", "gy")),
        P(None, None, "gz", ("gx", "gy")),
        P(None, "gz", ("gx", "gy")),
    )
    out_specs = (P(None, "gz", "gx", "gy"), P(None, "gz", "gx", "gy"), P(None, "gz", ("gx", "gy")))
    return jax.shard_map(body, mesh=mesh, in_specs=in_specs, out_specs=out_specs, check_vma=False)
```

```python
import functools

import jax
import jax.numpy as jnp
from jax import lax
from jax.experimental import pallas as pl
from jax.experimental.pallas import tpu as pltpu
from jax.sharding import PartitionSpec as P

MESH = pl.DeviceIdType.MESH
STEPS = 3
RELAX_TIME = 0.8
SPEED_SCALE = 0.05

VELOCITIES = [
    (0, 0, 0),
    (1, 0, 0),
    (-1, 0, 0),
    (0, 1, 0),
    (0, -1, 0),
    (0, 0, 1),
    (0, 0, -1),
    (1, 1, 0),
    (-1, -1, 0),
    (1, -1, 0),
    (-1, 1, 0),
    (1, 0, 1),
    (-1, 0, -1),
    (1, 0, -1),
    (-1, 0, 1),
    (0, 1, 1),
    (0, -1, -1),
    (0, 1, -1),
    (0, -1, 1),
]
INDEX = {vector: member for member, vector in enumerate(VELOCITIES)}
INPLANE = [
    (0, 0, 0),
    (0, 0, 1),
    (0, 0, -1),
    (0, 1, 0),
    (0, 1, 1),
    (0, 1, -1),
    (0, -1, 0),
    (0, -1, 1),
    (0, -1, -1),
]
AXIAL = [
    [(1, 0, 0), (1, 0, 1), (1, 0, -1), (1, 1, 0), (1, -1, 0)],
    [(-1, 0, 0), (-1, 0, 1), (-1, 0, -1), (-1, 1, 0), (-1, -1, 0)],
]
EDGES = [
    (0, 0, 1),
    (0, 0, -1),
    (0, 1, 1),
    (0, 1, -1),
    (0, -1, 1),
    (0, -1, -1),
    (1, 0, 1),
    (1, 0, -1),
    (-1, 0, 1),
    (-1, 0, -1),
]
DIAGONAL = [(0, 1, 1), (0, 1, -1), (0, -1, 1), (0, -1, -1)]

SIZE = 16
BLOCKS = 4
OUTER_BLOCKS = 1
OUTER_ROWS = SIZE * OUTER_BLOCKS
CENTRE_ROWS = SIZE * (BLOCKS - OUTER_BLOCKS)
SPAN = 128 // BLOCKS
N_AXIAL = 0
N_AXIAL_ROW = 4
N_ROW = 8
N_EDGE = 10
N_SAMPLE = 15
N_MESSAGES = 24


def tree_sum(values):
    while len(values) > 1:
        pairs = [values[i] + values[i + 1] for i in range(0, len(values) - 1, 2)]
        if len(values) % 2:
            pairs.append(values[-1])
        values = pairs
    return values[0]


def moments(f):
    density = tree_sum(f)
    inverse = 1.0 / density
    components = []
    for column in range(3):
        ahead = tree_sum([f[m] for m in range(19) if VELOCITIES[m][column] == 1])
        back = tree_sum([f[m] for m in range(19) if VELOCITIES[m][column] == -1])
        components.append((ahead - back) * inverse)
    return density, inverse, components


def dot(vector, u):
    total = None
    for c, x in zip(vector, u):
        if c == 0:
            continue
        if total is None:
            total = x if c == 1 else -x
        else:
            total = total + x if c == 1 else total - x
    return total


def collide(f, density, u, fluid):
    base = 1.0 - 1.5 * (u[0] * u[0] + u[1] * u[1] + u[2] * u[2])
    keep = 1.0 - 1.0 / RELAX_TIME
    scaled = density * (1.0 / RELAX_TIME)
    heavy = scaled * (1.0 / 18.0)
    light = scaled * (1.0 / 36.0)
    post = [None] * 19
    post[0] = jnp.where(fluid, scaled * (1.0 / 3.0) * base + keep * f[0], f[0])
    for m in range(1, 19, 2):
        weight = heavy if m < 7 else light
        projected = dot(VELOCITIES[m], u)
        even = weight * (base + 4.5 * (projected * projected))
        odd = (3.0 * weight) * projected
        post[m] = jnp.where(fluid, (even + odd) + keep * f[m], f[m + 1])
        post[m + 1] = jnp.where(fluid, (even - odd) + keep * f[m + 1], f[m])
    return post


def split(x):
    high = x.astype(jnp.bfloat16)
    low = (x - high.astype(jnp.float32)).astype(jnp.bfloat16)
    return high, low


def product(x, w_high, w_low, dims):
    high, low = split(x)
    one = functools.partial(
        lax.dot_general, dimension_numbers=(dims, ((), ())), preferred_element_type=jnp.float32
    )
    return one(high, w_high) + (one(low, w_high) + one(high, w_low))


def edge(value, packed, vector):
    j = EDGES.index(vector)
    lane = lax.broadcasted_iota(jnp.int32, value.shape, 1)
    if vector[2] == 1:
        there = packed if j == 0 else pltpu.roll(packed, 128 - j, 1)
        return jnp.where(lane == 0, there, value)
    return jnp.where(lane == 127, pltpu.roll(packed, 127 - j, 1), value)


def unpacked(packed, rb):
    return pltpu.roll(packed, lax.rem(128 - SPAN * rb, 128), 1)


def patch(pb, er, pp):
    def block(rb, carry):
        row = pl.multiple_of(rb * SIZE + 8, 8)
        packed = unpacked(er[0], rb)
        for k, vector in enumerate(DIAGONAL):
            value = pb[INPLANE.index(vector), pl.ds(row, SIZE), :]
            pp[k, pl.ds(row, SIZE), :] = edge(value, packed, vector)
        return carry

    lax.fori_loop(0, BLOCKS, block, 0, unroll=True)
    before = pltpu.roll(er[1, SIZE - 8 :, :], SPAN, 1)
    after = er[2, 0:8, :]
    for k, vector in enumerate(DIAGONAL):
        packed, row = (before, 0) if vector[1] == 1 else (after, 72)
        value = pb[INPLANE.index(vector), pl.ds(row, 8), :]
        pp[k, pl.ds(row, 8), :] = edge(value, packed, vector)


def streamed(pb, zr, er, pp, rb):
    row = pl.multiple_of(rb * SIZE, 8)
    packed = {0: unpacked(er[0], rb), 1: unpacked(er[3], rb), -1: unpacked(er[4], rb)}
    f = []
    for vector in VELOCITIES:
        rows = pl.ds(row + (8 - vector[1]), SIZE)
        if vector in DIAGONAL:
            f.append(pp[DIAGONAL.index(vector), rows, :])
            continue
        if vector[0] == 0:
            value = pb[INPLANE.index(vector), rows, :]
        else:
            way = 0 if vector[0] == 1 else 1
            value = zr[way, AXIAL[way].index(vector), rows, :]
        if vector[2] != 0:
            value = edge(value, packed[vector[0]], vector)
        f.append(value)
    return f


def kernel(
    gz_size,
    pops_in,
    solid_in,
    whirl_in,
    cells_in,
    weights_in,
    target_in,
    pb_last,
    zr_last,
    er_last,
    force_last,
    pb_early,
    zs,
    zr_early,
    es,
    er_early,
    pp,
    st,
    mom,
    fb,
    mk_own,
    mk_all,
    mk,
    sp,
    wx,
    wy_high,
    wy_low,
    send_sem,
    recv_sem,
    mk_send,
    mk_recv,
    pops,
    solid,
    whirl,
    cells,
    weights,
    target,
    load_sem,
):
    loads = [
        pltpu.make_async_copy(src, dst, load_sem.at[k])
        for k, (src, dst) in enumerate(
            [
                (cells_in, cells),
                (weights_in, weights),
                (target_in, target),
                (whirl_in, whirl),
                (pops_in, pops),
                (solid_in, solid),
            ]
        )
    ]
    for load in loads:
        load.start()
    pb = [pb_early.at[s] for s in range(STEPS - 1)] + [pb_last]
    zr = [zr_early.at[s] for s in range(STEPS - 1)] + [zr_last]
    er = [er_early.at[s] for s in range(STEPS - 1)] + [er_last]
    gz = lax.axis_index("gz")
    gx = lax.axis_index("gx")
    gy = lax.axis_index("gy")
    z_next, z_prev = lax.rem(gz + 1, gz_size), lax.rem(gz + gz_size - 1, gz_size)
    x_next, x_prev, x_far = lax.rem(gx + 1, 4), lax.rem(gx + 3, 4), lax.rem(gx + 2, 4)
    y_other = 1 - gy
    flip = gx // 2
    is_centre = lax.rem((gx + 1) // 2, 2)
    centre = is_centre == 1
    outer = is_centre == 0
    quarter = lax.rem(2 * gx + gy + 2, 4)
    own = 2 * gx + gy
    outer_start = pl.multiple_of(CENTRE_ROWS * flip, 8)
    centre_start = pl.multiple_of(OUTER_ROWS * (1 - flip), 8)

    barrier = pltpu.get_barrier_semaphore()
    neighbours = [
        {"gz": gz, "gx": x_next, "gy": gy},
        {"gz": gz, "gx": x_prev, "gy": gy},
        {"gz": gz, "gx": x_far, "gy": gy},
        {"gz": gz, "gx": gx, "gy": y_other},
        {"gz": gz, "gx": x_next, "gy": y_other},
        {"gz": gz, "gx": x_prev, "gy": y_other},
        {"gz": gz, "gx": x_far, "gy": y_other},
    ]
    for z in (z_next, z_prev):
        neighbours += [
            {"gz": z, "gx": gx, "gy": gy},
            {"gz": z, "gx": x_next, "gy": gy},
            {"gz": z, "gx": x_prev, "gy": gy},
            {"gz": z, "gx": gx, "gy": y_other},
        ]
    for place in neighbours:
        pl.semaphore_signal(barrier, inc=1, device_id=place, device_id_type=MESH)

    lanes = lax.broadcasted_iota(jnp.int32, (SIZE, 128), 1)
    lane_block = lanes // SPAN

    def block_of(b):
        return b + flip * (BLOCKS - 1 - 2 * b)

    def remote(src, dst, s, n, place, n_recv=None):
        return pltpu.make_async_remote_copy(
            src_ref=src,
            dst_ref=dst,
            send_sem=send_sem.at[s, n],
            recv_sem=recv_sem.at[s, n if n_recv is None else n_recv],
            device_id=place,
            device_id_type=MESH,
        )

    def axial(s, way, part):
        start, size = ((outer_start, OUTER_ROWS), (centre_start, CENTRE_ROWS))[part]
        return remote(
            zs.at[s, way, :, pl.ds(start, size), :],
            zr[s].at[way, :, pl.ds(pl.multiple_of(start + 8, 8), size), :],
            s,
            N_AXIAL + 2 * way + part,
            {"gz": (z_next, z_prev)[way], "gx": gx, "gy": gy},
        )

    def small(s):
        copies = []
        for way in range(2):
            z = (z_next, z_prev)[way]
            copies.append(
                remote(
                    zs.at[s, way, 3, pl.ds(56, 8), :],
                    zr[s].at[way, 3, pl.ds(0, 8), :],
                    s,
                    N_AXIAL_ROW + 2 * way,
                    {"gz": z, "gx": x_next, "gy": gy},
                )
            )
            copies.append(
                remote(
                    zs.at[s, way, 4, pl.ds(0, 8), :],
                    zr[s].at[way, 4, pl.ds(72, 8), :],
                    s,
                    N_AXIAL_ROW + 2 * way + 1,
                    {"gz": z, "gx": x_prev, "gy": gy},
                )
            )
        copies.append(
            remote(
                pb[s].at[pl.ds(3, 3), pl.ds(64, 8), :],
                pb[s].at[pl.ds(3, 3), pl.ds(0, 8), :],
                s,
                N_ROW,
                {"gz": gz, "gx": x_next, "gy": gy},
            )
        )
        copies.append(
            remote(
                pb[s].at[pl.ds(6, 3), pl.ds(8, 8), :],
                pb[s].at[pl.ds(6, 3), pl.ds(72, 8), :],
                s,
                N_ROW + 1,
                {"gz": gz, "gx": x_prev, "gy": gy},
            )
        )
        places = [
            {"gz": gz, "gx": gx, "gy": y_other},
            {"gz": gz, "gx": x_next, "gy": y_other},
            {"gz": gz, "gx": x_prev, "gy": y_other},
            {"gz": z_next, "gx": gx, "gy": y_other},
            {"gz": z_prev, "gx": gx, "gy": y_other},
        ]
        for k, place in enumerate(places):
            copies.append(remote(es.at[s], er[s].at[k], s, N_EDGE + k, place))
        return copies

    def sample_copies(s):
        pair = 3 - gx
        places = [(gx, y_other), (pair, gy), (pair, y_other)]
        if s == STEPS - 1:
            places += [(0, gy), (0, y_other), (3, gy), (3, y_other)]
        return [
            remote(
                sp.at[s, quarter],
                sp.at[s, quarter],
                s,
                N_SAMPLE + d,
                {"gz": gz, "gx": x, "gy": y},
                N_SAMPLE + quarter,
            )
            for d, (x, y) in enumerate(places)
        ]

    def sample_wait(s, q):
        remote(sp.at[s, q], sp.at[s, q], s, N_SAMPLE, neighbours[0], N_SAMPLE + q).wait_recv()

    def centre_place(t):
        return {"gz": gz, "gx": 1 + t // 2, "gy": t % 2}

    def marker_copy(t):
        return pltpu.make_async_remote_copy(
            src_ref=mk_all.at[own],
            dst_ref=mk_all.at[own],
            send_sem=mk_send.at[t],
            recv_sem=mk_recv.at[own],
            device_id=centre_place(t),
            device_id_type=MESH,
        )

    def marker_wait(j):
        pltpu.make_async_remote_copy(
            src_ref=mk_all.at[j],
            dst_ref=mk_all.at[j],
            send_sem=mk_send.at[0],
            recv_sem=mk_recv.at[j],
            device_id=neighbours[0],
            device_id_type=MESH,
        ).wait_recv()

    def not_self(t):
        return jnp.logical_or(gx != 1 + t // 2, gy != t % 2)

    def gather(s, rb):
        if s == 0:
            row = pl.multiple_of(rb * SIZE, 8)
            return [pops[m, 0, pl.ds(row, SIZE), :] for m in range(19)]
        return streamed(pb[s - 1], zr[s - 1], er[s - 1], pp, rb)

    def store_post(s, rb, post):
        row = pl.multiple_of(rb * SIZE, 8)
        for vector in VELOCITIES:
            value = post[INDEX[vector]]
            if vector[2] != 0:
                value = pltpu.roll(value, 1 if vector[2] == 1 else 127, 1)
            if vector[0] == 0:
                pb[s][INPLANE.index(vector), pl.ds(pl.multiple_of(row + 8, 8), SIZE), :] = value
            else:
                way = 0 if vector[0] == 1 else 1
                zs[s, way, AXIAL[way].index(vector), pl.ds(row, SIZE), :] = value
        packed = post[INDEX[EDGES[0]]]
        packed = pltpu.roll(packed, 1, 1)
        for j, vector in enumerate(EDGES):
            if j == 0:
                continue
            shift = j + 1 if vector[2] == 1 else j
            packed = jnp.where(lanes == j, pltpu.roll(post[INDEX[vector]], shift, 1), packed)
        es[s] = jnp.where(lane_block == rb, pltpu.roll(packed, SPAN * rb, 1), es[s])

    def fluid_of(rb):
        return solid[0, pl.ds(pl.multiple_of(rb * SIZE, 8), SIZE), :] == 0

    def whole_block(s):
        def block(b, carry):
            rb = block_of(b)
            f = gather(s, rb)
            density, _, u = moments(f)
            store_post(s, rb, collide(f, density, u, fluid_of(rb)))
            return carry

        return block

    def first_half(s):
        def block(b, carry):
            rb = block_of(b)
            row = pl.multiple_of(rb * SIZE, 8)
            f = gather(s, rb)
            density, inverse, u = moments(f)
            if s > 0:
                for m in range(19):
                    st[m, pl.ds(row, SIZE), :] = f[m]
            for c, value in enumerate([*u, density, inverse]):
                mom[c, pl.ds(row, SIZE), :] = value
            return carry

        return block

    def second_half(s):
        def block(b, carry):
            rb = block_of(b)
            row = pl.multiple_of(rb * SIZE, 8)
            if s == 0:
                f = [pops[m, 0, pl.ds(row, SIZE), :] for m in range(19)]
            else:
                f = [st[m, pl.ds(row, SIZE), :] for m in range(19)]
            density = mom[3, pl.ds(row, SIZE), :]
            scale = RELAX_TIME * mom[4, pl.ds(row, SIZE), :]
            near = pl.multiple_of(row - centre_start, 8)
            u = [mom[c, pl.ds(row, SIZE), :] + scale * fb[c, pl.ds(near, SIZE), :] for c in range(3)]
            store_post(s, rb, collide(f, density, u, fluid_of(rb)))
            return carry

        return block

    def marker_matrices(s):
        def matrix(size, first, base, row):
            place = lax.broadcasted_iota(jnp.int32, (size, 256), 0) + first
            distance = place.astype(jnp.float32) - base
            result = jnp.zeros((size, 256), jnp.float32)
            for a in range(4):
                result = jnp.where(distance == float(a), mk[row + a : row + a + 1, :], result)
            return result

        base_x = mk[0:1, :] + (127 + whirl[0, s]).astype(jnp.float32)
        base_y = mk[1:2, :] + (127 + whirl[1, s]).astype(jnp.float32)
        wx[...] = matrix(CENTRE_ROWS, 64 * gx + centre_start, base_x, 2)
        high, low = split(matrix(128, 128 * gy, base_y, 6))
        wy_high[...] = high
        wy_low[...] = low

    def sample(s):
        u = mom[0:3, pl.ds(centre_start, CENTRE_ROWS), :].reshape(3 * CENTRE_ROWS, 128)
        along = product(u, wy_high[...], wy_low[...], ((1,), (0,)))
        spread = wx[...]
        rows = [
            jnp.sum(along[c * CENTRE_ROWS : (c + 1) * CENTRE_ROWS] * spread, axis=0, keepdims=True)
            for c in range(3)
        ]
        sp[s, quarter] = jnp.concatenate(rows + [jnp.zeros((5, 256), jnp.float32)], axis=0)

    def sampled(s):
        return (sp[s, 0] + sp[s, 1]) + (sp[s, 2] + sp[s, 3])

    def force(s):
        push = mk[10:13, :] - sampled(s)[0:3, :]
        spread = wx[...]
        weighted = jnp.concatenate([spread * push[c : c + 1, :] for c in range(3)], axis=0)
        body = product(weighted, wy_high[...], wy_low[...], ((1,), (1,)))
        fb[...] = body.reshape(3, CENTRE_ROWS, 128)

    for load in loads[:4]:
        load.wait()
    mk_own[...] = jnp.zeros((16, 128), jnp.float32)
    mk_own[0:2, 0:32] = cells[:, 0, :].astype(jnp.float32)
    mk_own[2:6, 0:32] = weights[0, :, 0, :]
    mk_own[6:10, 0:32] = weights[1, :, 0, :]
    mk_own[10:13, 0:32] = target[:, 0, :]
    mk_all[own] = pltpu.roll(mk_own[...], 32 * lax.rem(own, 4), 1)

    pl.semaphore_wait(barrier, len(neighbours))

    for t in range(4):

        @pl.when(not_self(t))
        def _(t=t):
            marker_copy(t).start()

    for load in loads[4:]:
        load.wait()

    for s in range(STEPS):
        last = s == STEPS - 1
        if s > 0:
            for copy in [axial(s - 1, way, part) for way in range(2) for part in range(2)] + small(s - 1):
                copy.wait_recv()
            patch(pb[s - 1], er[s - 1], pp)

        @pl.when(centre)
        def _(s=s):
            lax.fori_loop(OUTER_BLOCKS, BLOCKS, first_half(s), 0, unroll=True)
            if s == 0:
                for d in range(1, 8):
                    marker_wait(lax.rem(own + d, 8))
                mk[:, 0:128] = (mk_all[0] + mk_all[1]) + (mk_all[2] + mk_all[3])
                mk[:, 128:256] = (mk_all[4] + mk_all[5]) + (mk_all[6] + mk_all[7])
                marker_matrices(s)
            sample(s)
            for copy in sample_copies(s):
                copy.start()

        lax.fori_loop(0, OUTER_BLOCKS, whole_block(s), 0, unroll=True)
        for way in range(2):
            axial(s, way, 0).start()

        @pl.when(outer)
        def _(s=s):
            lax.fori_loop(OUTER_BLOCKS, BLOCKS, whole_block(s), 0, unroll=True)

        @pl.when(centre)
        def _(s=s):
            for d in range(1, 4):
                sample_wait(s, lax.rem(quarter + d, 4))
            force(s)
            lax.fori_loop(OUTER_BLOCKS, BLOCKS, second_half(s), 0, unroll=True)

        for copy in small(s)[::-1]:
            copy.start()
        for way in range(2):
            axial(s, way, 1).start()

        if not last:

            @pl.when(centre)
            def _(s=s):
                marker_matrices(s + 1)

    for copy in [axial(STEPS - 1, way, part) for way in range(2) for part in range(2)] + small(STEPS - 1):
        copy.wait_recv()

    @pl.when(outer)
    def _():
        for q in range(4):
            sample_wait(STEPS - 1, q)

    total = sampled(STEPS - 1)
    half = jnp.where(own // 4 == 0, total[:, 0:128], total[:, 128:256])
    half = pltpu.roll(half, lax.rem(128 - 32 * lax.rem(own, 4), 128), 1)
    force_last[:, 0, :] = (target[:, 0, :] - half[0:3, 0:32]) * (1.0 / SPEED_SCALE)

    for t in range(4):

        @pl.when(not_self(t))
        def _(t=t):
            marker_copy(t).wait_send()

    for s in range(STEPS):
        for copy in [axial(s, way, part) for way in range(2) for part in range(2)] + small(s):
            copy.wait_send()

    @pl.when(centre)
    def _():
        for s in range(STEPS):
            for copy in sample_copies(s):
                copy.wait_send()


def finish(pb, zr, er, force, solid, res_pops, res_vel, res_force, pp, out_pops, out_vel, sem):
    patch(pb, er, pp)
    copies = []
    for rb in range(BLOCKS):
        rows = pl.ds(rb * SIZE, SIZE)
        f = streamed(pb, zr, er, pp, rb)
        for m in range(19):
            out_pops[m, 0, rows, :] = f[m]
        _, _, u = moments(f)
        fluid = solid[0, rows, :] == 0
        for c in range(3):
            out_vel[c, 0, rows, :] = jnp.where(fluid, u[c] * (1.0 / SPEED_SCALE), 0.0)
        for k, (src, dst) in enumerate([(out_pops, res_pops), (out_vel, res_vel)]):
            copy = pltpu.make_async_copy(
                src.at[:, :, rows, :], dst.at[:, :, rows, :], sem.at[2 * rb + k]
            )
            copy.start()
            copies.append(copy)
    copy = pltpu.make_async_copy(force, res_force, sem.at[2 * BLOCKS])
    copy.start()
    copies.append(copy)
    for copy in copies:
        copy.wait()


def body(populations, solid_mask, whirl_offsets, marker_cells, marker_weights, pipe_velocity):
    f32 = jnp.float32
    vmem = pl.BlockSpec(memory_space=pltpu.VMEM)
    hbm = pl.BlockSpec(memory_space=pltpu.HBM)
    pb, zr, er = (9, 80, 128), (2, 5, 80, 128), (5, SIZE, 128)
    arrived = pl.pallas_call(
        functools.partial(kernel, lax.axis_size("gz")),
        out_shape=[pltpu.VMEM(shape, f32) for shape in (pb, zr, er, pipe_velocity.shape)],
        in_specs=[hbm] * 6,
        out_specs=[vmem] * 4,
        scratch_shapes=[
            pltpu.VMEM((STEPS - 1,) + pb, f32),
            pltpu.VMEM((STEPS, 2, 5, 64, 128), f32),
            pltpu.VMEM((STEPS - 1,) + zr, f32),
            pltpu.VMEM((STEPS, SIZE, 128), f32),
            pltpu.VMEM((STEPS - 1,) + er, f32),
            pltpu.VMEM((4, 80, 128), f32),
            pltpu.VMEM((19, 64, 128), f32),
            pltpu.VMEM((5, 64, 128), f32),
            pltpu.VMEM((3, CENTRE_ROWS, 128), f32),
            pltpu.VMEM((16, 128), f32),
            pltpu.VMEM((8, 16, 128), f32),
            pltpu.VMEM((16, 256), f32),
            pltpu.VMEM((STEPS, 4, 8, 256), f32),
            pltpu.VMEM((CENTRE_ROWS, 256), f32),
            pltpu.VMEM((128, 256), jnp.bfloat16),
            pltpu.VMEM((128, 256), jnp.bfloat16),
            pltpu.SemaphoreType.DMA((STEPS, N_MESSAGES)),
            pltpu.SemaphoreType.DMA((STEPS, N_MESSAGES)),
            pltpu.SemaphoreType.DMA((4,)),
            pltpu.SemaphoreType.DMA((8,)),
            pltpu.VMEM(populations.shape, f32),
            pltpu.VMEM(solid_mask.shape, jnp.int32),
            pltpu.SMEM(whirl_offsets.shape[::-1], jnp.int32),
            pltpu.VMEM(marker_cells.shape, jnp.int32),
            pltpu.VMEM(marker_weights.shape, f32),
            pltpu.VMEM(pipe_velocity.shape, f32),
            pltpu.SemaphoreType.DMA((6,)),
        ],
        compiler_params=pltpu.CompilerParams(
            collective_id=0, has_side_effects=True, vmem_limit_bytes=60 * 1024 * 1024
        ),
        cost_estimate=pl.CostEstimate(flops=40_000_000, bytes_accessed=2_000_000, transcendentals=0),
    )(populations, solid_mask, whirl_offsets.T, marker_cells, marker_weights, pipe_velocity)
    shapes = (populations.shape, (3,) + solid_mask.shape, pipe_velocity.shape)
    return pl.pallas_call(
        finish,
        out_shape=[jax.ShapeDtypeStruct(shape, f32) for shape in shapes],
        in_specs=[vmem] * 5,
        out_specs=[hbm] * 3,
        scratch_shapes=[pltpu.VMEM((4, 80, 128), f32)]
        + [pltpu.VMEM(shape, f32) for shape in shapes[:2]]
        + [pltpu.SemaphoreType.DMA((2 * BLOCKS + 1,))],
        compiler_params=pltpu.CompilerParams(vmem_limit_bytes=24 * 1024 * 1024),
        cost_estimate=pl.CostEstimate(flops=2_000_000, bytes_accessed=2_000_000, transcendentals=0),
    )(*arrived, solid_mask)


def solution(mesh):
    in_specs = (
        P(None, "gz", "gx", "gy"),
        P("gz", "gx", "gy"),
        P(),
        P(None, "gz", ("gx", "gy")),
        P(None, None, "gz", ("gx", "gy")),
        P(None, "gz", ("gx", "gy")),
    )
    out_specs = (P(None, "gz", "gx", "gy"), P(None, "gz", "gx", "gy"), P(None, "gz", ("gx", "gy")))
    return jax.shard_map(body, mesh=mesh, in_specs=in_specs, out_specs=out_specs, check_vma=False)
```

```python
import functools

import jax
import jax.numpy as jnp
from jax import lax
from jax.experimental import pallas as pl
from jax.experimental.pallas import tpu as pltpu
from jax.sharding import PartitionSpec as P

MESH = pl.DeviceIdType.MESH
STEPS = 3
RELAX_TIME = 0.8
SPEED_SCALE = 0.05

VELOCITIES = [
    (0, 0, 0),
    (1, 0, 0),
    (-1, 0, 0),
    (0, 1, 0),
    (0, -1, 0),
    (0, 0, 1),
    (0, 0, -1),
    (1, 1, 0),
    (-1, -1, 0),
    (1, -1, 0),
    (-1, 1, 0),
    (1, 0, 1),
    (-1, 0, -1),
    (1, 0, -1),
    (-1, 0, 1),
    (0, 1, 1),
    (0, -1, -1),
    (0, 1, -1),
    (0, -1, 1),
]
INDEX = {vector: member for member, vector in enumerate(VELOCITIES)}
INPLANE = [
    (0, 0, 0),
    (0, 0, 1),
    (0, 0, -1),
    (0, 1, 0),
    (0, 1, 1),
    (0, 1, -1),
    (0, -1, 0),
    (0, -1, 1),
    (0, -1, -1),
]
AXIAL = [
    [(1, 0, 0), (1, 0, 1), (1, 0, -1), (1, 1, 0), (1, -1, 0)],
    [(-1, 0, 0), (-1, 0, 1), (-1, 0, -1), (-1, 1, 0), (-1, -1, 0)],
]
EDGES = [
    (0, 0, 1),
    (0, 0, -1),
    (0, 1, 1),
    (0, 1, -1),
    (0, -1, 1),
    (0, -1, -1),
    (1, 0, 1),
    (1, 0, -1),
    (-1, 0, 1),
    (-1, 0, -1),
]
DIAGONAL = [(0, 1, 1), (0, 1, -1), (0, -1, 1), (0, -1, -1)]

SIZE = 16
BLOCKS = 4
OUTER_BLOCKS = 1
OUTER_ROWS = SIZE * OUTER_BLOCKS
CENTRE_ROWS = SIZE * (BLOCKS - OUTER_BLOCKS)
SPAN = 128 // BLOCKS
N_AXIAL = 0
N_AXIAL_ROW = 4
N_ROW = 8
N_EDGE = 10
N_SAMPLE = 15
N_STRIP = 22
N_MESSAGES = 24


def tree_sum(values):
    while len(values) > 1:
        pairs = [values[i] + values[i + 1] for i in range(0, len(values) - 1, 2)]
        if len(values) % 2:
            pairs.append(values[-1])
        values = pairs
    return values[0]


def moments(f):
    density = tree_sum(f)
    inverse = 1.0 / density
    components = []
    for column in range(3):
        ahead = tree_sum([f[m] for m in range(19) if VELOCITIES[m][column] == 1])
        back = tree_sum([f[m] for m in range(19) if VELOCITIES[m][column] == -1])
        components.append((ahead - back) * inverse)
    return density, inverse, components


def dot(vector, u):
    total = None
    for c, x in zip(vector, u):
        if c == 0:
            continue
        if total is None:
            total = x if c == 1 else -x
        else:
            total = total + x if c == 1 else total - x
    return total


def collide(f, density, u, fluid):
    base = 1.0 - 1.5 * (u[0] * u[0] + u[1] * u[1] + u[2] * u[2])
    keep = 1.0 - 1.0 / RELAX_TIME
    scaled = density * (1.0 / RELAX_TIME)
    heavy = scaled * (1.0 / 18.0)
    light = scaled * (1.0 / 36.0)
    post = [None] * 19
    post[0] = jnp.where(fluid, scaled * (1.0 / 3.0) * base + keep * f[0], f[0])
    for m in range(1, 19, 2):
        weight = heavy if m < 7 else light
        projected = dot(VELOCITIES[m], u)
        even = weight * (base + 4.5 * (projected * projected))
        odd = (3.0 * weight) * projected
        post[m] = jnp.where(fluid, (even + odd) + keep * f[m], f[m + 1])
        post[m + 1] = jnp.where(fluid, (even - odd) + keep * f[m + 1], f[m])
    return post


def split(x):
    high = x.astype(jnp.bfloat16)
    low = (x - high.astype(jnp.float32)).astype(jnp.bfloat16)
    return high, low


def product(x, w_high, w_low, dims):
    high, low = split(x)
    one = functools.partial(
        lax.dot_general, dimension_numbers=(dims, ((), ())), preferred_element_type=jnp.float32
    )
    return one(high, w_high) + (one(low, w_high) + one(high, w_low))


def edge(value, packed, vector):
    j = EDGES.index(vector)
    lane = lax.broadcasted_iota(jnp.int32, value.shape, 1)
    if vector[2] == 1:
        there = packed if j == 0 else pltpu.roll(packed, 128 - j, 1)
        return jnp.where(lane == 0, there, value)
    return jnp.where(lane == 127, pltpu.roll(packed, 127 - j, 1), value)


def unpacked(packed, rb):
    return pltpu.roll(packed, lax.rem(128 - SPAN * rb, 128), 1)


def patch(pb, er, pp):
    def block(rb, carry):
        row = pl.multiple_of(rb * SIZE + 8, 8)
        packed = unpacked(er[0], rb)
        for k, vector in enumerate(DIAGONAL):
            value = pb[INPLANE.index(vector), pl.ds(row, SIZE), :]
            pp[k, pl.ds(row, SIZE), :] = edge(value, packed, vector)
        return carry

    lax.fori_loop(0, BLOCKS, block, 0, unroll=True)
    before = pltpu.roll(er[1, SIZE - 8 :, :], SPAN, 1)
    after = er[2, 0:8, :]
    for k, vector in enumerate(DIAGONAL):
        packed, row = (before, 0) if vector[1] == 1 else (after, 72)
        value = pb[INPLANE.index(vector), pl.ds(row, 8), :]
        pp[k, pl.ds(row, 8), :] = edge(value, packed, vector)


def streamed(pb, zr, er, pp, rb):
    row = pl.multiple_of(rb * SIZE, 8)
    packed = {0: unpacked(er[0], rb), 1: unpacked(er[3], rb), -1: unpacked(er[4], rb)}
    f = []
    for vector in VELOCITIES:
        rows = pl.ds(row + (8 - vector[1]), SIZE)
        if vector in DIAGONAL:
            f.append(pp[DIAGONAL.index(vector), rows, :])
            continue
        if vector[0] == 0:
            value = pb[INPLANE.index(vector), rows, :]
        else:
            way = 0 if vector[0] == 1 else 1
            value = zr[way, AXIAL[way].index(vector), rows, :]
        if vector[2] != 0:
            value = edge(value, packed[vector[0]], vector)
        f.append(value)
    return f


def kernel(
    gz_size,
    pops_in,
    solid_in,
    whirl_in,
    cells_in,
    weights_in,
    target_in,
    pb_last,
    zr_last,
    er_last,
    force_last,
    pb_early,
    zs,
    zr_early,
    es,
    er_early,
    pp,
    st,
    mom,
    fb,
    mk_own,
    mk_all,
    mk,
    sp,
    wx,
    wy_high,
    wy_low,
    send_sem,
    recv_sem,
    mk_send,
    mk_recv,
    pops,
    solid,
    whirl,
    cells,
    weights,
    target,
    strip_out,
    strip_in,
    rows_in,
    full,
    load_sem,
    vouch_sem,
):
    loads = [
        pltpu.make_async_copy(src, dst, load_sem.at[k])
        for k, (src, dst) in enumerate(
            [
                (cells_in, cells),
                (weights_in, weights),
                (target_in, target),
                (whirl_in, whirl),
                (pops_in, pops),
                (solid_in, solid),
            ]
        )
    ]
    for load in loads:
        load.start()
    pb = [pb_early.at[s] for s in range(STEPS - 1)] + [pb_last]
    zr = [zr_early.at[s] for s in range(STEPS - 1)] + [zr_last]
    er = [er_early.at[s] for s in range(STEPS - 1)] + [er_last]
    gz = lax.axis_index("gz")
    gx = lax.axis_index("gx")
    gy = lax.axis_index("gy")
    z_next, z_prev = lax.rem(gz + 1, gz_size), lax.rem(gz + gz_size - 1, gz_size)
    x_next, x_prev, x_far = lax.rem(gx + 1, 4), lax.rem(gx + 3, 4), lax.rem(gx + 2, 4)
    y_other = 1 - gy
    flip = gx // 2
    is_centre = lax.rem((gx + 1) // 2, 2)
    centre = is_centre == 1
    outer = is_centre == 0
    quarter = lax.rem(2 * gx + gy + 2, 4)
    own = 2 * gx + gy
    outer_start = pl.multiple_of(CENTRE_ROWS * flip, 8)
    centre_start = pl.multiple_of(OUTER_ROWS * (1 - flip), 8)

    barrier = pltpu.get_barrier_semaphore()
    neighbours = [
        {"gz": gz, "gx": x_next, "gy": gy},
        {"gz": gz, "gx": x_prev, "gy": gy},
        {"gz": gz, "gx": x_far, "gy": gy},
        {"gz": gz, "gx": gx, "gy": y_other},
        {"gz": gz, "gx": x_next, "gy": y_other},
        {"gz": gz, "gx": x_prev, "gy": y_other},
        {"gz": gz, "gx": x_far, "gy": y_other},
    ]
    for z in (z_next, z_prev):
        neighbours.append({"gz": z, "gx": gx, "gy": gy})
    for place in neighbours:
        pl.semaphore_signal(barrier, inc=1, device_id=place, device_id_type=MESH)

    lanes = lax.broadcasted_iota(jnp.int32, (SIZE, 128), 1)
    lane_block = lanes // SPAN

    def block_of(b):
        return b + flip * (BLOCKS - 1 - 2 * b)

    def remote(src, dst, s, n, place, n_recv=None):
        return pltpu.make_async_remote_copy(
            src_ref=src,
            dst_ref=dst,
            send_sem=send_sem.at[s, n],
            recv_sem=recv_sem.at[s, n if n_recv is None else n_recv],
            device_id=place,
            device_id_type=MESH,
        )

    def axial(s, way, part):
        start, size = ((outer_start, OUTER_ROWS), (centre_start, CENTRE_ROWS))[part]
        return remote(
            zs.at[s, way, :, pl.ds(start, size), :],
            zr[s].at[way, :, pl.ds(pl.multiple_of(start + 8, 8), size), :],
            s,
            N_AXIAL + 2 * way + part,
            {"gz": (z_next, z_prev)[way], "gx": gx, "gy": gy},
        )

    def small(s):
        copies = []
        for way in range(2):
            z = (z_next, z_prev)[way]
            copies.append(
                remote(
                    zs.at[s, way, 3, pl.ds(56, 8), :],
                    zr[s].at[way, 3, pl.ds(0, 8), :],
                    s,
                    N_AXIAL_ROW + 2 * way,
                    {"gz": z, "gx": x_next, "gy": gy},
                )
            )
            copies.append(
                remote(
                    zs.at[s, way, 4, pl.ds(0, 8), :],
                    zr[s].at[way, 4, pl.ds(72, 8), :],
                    s,
                    N_AXIAL_ROW + 2 * way + 1,
                    {"gz": z, "gx": x_prev, "gy": gy},
                )
            )
        copies.append(
            remote(
                pb[s].at[pl.ds(3, 3), pl.ds(64, 8), :],
                pb[s].at[pl.ds(3, 3), pl.ds(0, 8), :],
                s,
                N_ROW,
                {"gz": gz, "gx": x_next, "gy": gy},
            )
        )
        copies.append(
            remote(
                pb[s].at[pl.ds(6, 3), pl.ds(8, 8), :],
                pb[s].at[pl.ds(6, 3), pl.ds(72, 8), :],
                s,
                N_ROW + 1,
                {"gz": gz, "gx": x_prev, "gy": gy},
            )
        )
        places = [
            {"gz": gz, "gx": gx, "gy": y_other},
            {"gz": gz, "gx": x_next, "gy": y_other},
            {"gz": gz, "gx": x_prev, "gy": y_other},
            {"gz": z_next, "gx": gx, "gy": y_other},
            {"gz": z_prev, "gx": gx, "gy": y_other},
        ]
        for k, place in enumerate(places):
            copies.append(remote(es.at[s], er[s].at[k], s, N_EDGE + k, place))
        return copies

    def sample_copies(s):
        pair = 3 - gx
        places = [(gx, y_other), (pair, gy), (pair, y_other)]
        if s == STEPS - 1:
            places += [(0, gy), (0, y_other), (3, gy), (3, y_other)]
        return [
            remote(
                sp.at[s, quarter],
                sp.at[s, quarter],
                s,
                N_SAMPLE + d,
                {"gz": gz, "gx": x, "gy": y},
                N_SAMPLE + quarter,
            )
            for d, (x, y) in enumerate(places)
        ]

    def sample_wait(s, q):
        remote(sp.at[s, q], sp.at[s, q], s, N_SAMPLE, neighbours[0], N_SAMPLE + q).wait_recv()

    def strip_copies():
        edge_rows = pl.ds(pl.multiple_of(56 - 56 * flip, 8), 8)
        return [
            remote(
                mom.at[pl.ds(0, 3), edge_rows, :],
                rows_in,
                0,
                N_STRIP,
                {"gz": gz, "gx": 3 - gx, "gy": gy},
            ),
            remote(strip_out, strip_in, 0, N_STRIP + 1, {"gz": gz, "gx": gx, "gy": y_other}),
        ]

    def centre_place(t):
        return {"gz": gz, "gx": 1 + t // 2, "gy": t % 2}

    def marker_copy(t):
        return pltpu.make_async_remote_copy(
            src_ref=mk_all.at[own],
            dst_ref=mk_all.at[own],
            send_sem=mk_send.at[t],
            recv_sem=mk_recv.at[own],
            device_id=centre_place(t),
            device_id_type=MESH,
        )

    def marker_wait(j):
        pltpu.make_async_remote_copy(
            src_ref=mk_all.at[j],
            dst_ref=mk_all.at[j],
            send_sem=mk_send.at[0],
            recv_sem=mk_recv.at[j],
            device_id=neighbours[0],
            device_id_type=MESH,
        ).wait_recv()

    def not_self(t):
        return jnp.logical_or(gx != 1 + t // 2, gy != t % 2)

    def gather(s, rb):
        if s == 0:
            row = pl.multiple_of(rb * SIZE, 8)
            return [pops[m, 0, pl.ds(row, SIZE), :] for m in range(19)]
        return streamed(pb[s - 1], zr[s - 1], er[s - 1], pp, rb)

    def store_post(s, rb, post):
        row = pl.multiple_of(rb * SIZE, 8)
        for vector in VELOCITIES:
            value = post[INDEX[vector]]
            if vector[2] != 0:
                value = pltpu.roll(value, 1 if vector[2] == 1 else 127, 1)
            if vector[0] == 0:
                pb[s][INPLANE.index(vector), pl.ds(pl.multiple_of(row + 8, 8), SIZE), :] = value
            else:
                way = 0 if vector[0] == 1 else 1
                zs[s, way, AXIAL[way].index(vector), pl.ds(row, SIZE), :] = value
        packed = post[INDEX[EDGES[0]]]
        packed = pltpu.roll(packed, 1, 1)
        for j, vector in enumerate(EDGES):
            if j == 0:
                continue
            shift = j + 1 if vector[2] == 1 else j
            packed = jnp.where(lanes == j, pltpu.roll(post[INDEX[vector]], shift, 1), packed)
        es[s] = jnp.where(lane_block == rb, pltpu.roll(packed, SPAN * rb, 1), es[s])

    def fluid_of(rb):
        return solid[0, pl.ds(pl.multiple_of(rb * SIZE, 8), SIZE), :] == 0

    def whole_block(s):
        def block(b, carry):
            rb = block_of(b)
            f = gather(s, rb)
            density, _, u = moments(f)
            store_post(s, rb, collide(f, density, u, fluid_of(rb)))
            return carry

        return block

    def first_half(s):
        def block(b, carry):
            rb = block_of(b)
            row = pl.multiple_of(rb * SIZE, 8)
            f = gather(s, rb)
            density, inverse, u = moments(f)
            if s > 0:
                for m in range(19):
                    st[m, pl.ds(row, SIZE), :] = f[m]
            for c, value in enumerate([*u, density, inverse]):
                mom[c, pl.ds(row, SIZE), :] = value
            return carry

        return block

    def second_half(s):
        def block(b, carry):
            rb = block_of(b)
            row = pl.multiple_of(rb * SIZE, 8)
            if s == 0:
                f = [pops[m, 0, pl.ds(row, SIZE), :] for m in range(19)]
            else:
                f = [st[m, pl.ds(row, SIZE), :] for m in range(19)]
            density = mom[3, pl.ds(row, SIZE), :]
            scale = RELAX_TIME * mom[4, pl.ds(row, SIZE), :]
            near = pl.multiple_of(row - centre_start, 8)
            u = [mom[c, pl.ds(row, SIZE), :] + scale * fb[c, pl.ds(near, SIZE), :] for c in range(3)]
            store_post(s, rb, collide(f, density, u, fluid_of(rb)))
            return carry

        return block

    def matrix(s, size, first, dim):
        base = mk[dim : dim + 1, :] + (127 + whirl[dim, s]).astype(jnp.float32)
        place = lax.broadcasted_iota(jnp.int32, (size, 256), 0) + first
        distance = place.astype(jnp.float32) - base
        result = jnp.zeros((size, 256), jnp.float32)
        for a in range(4):
            row = 2 + 4 * dim + a
            result = jnp.where(distance == float(a), mk[row : row + 1, :], result)
        return result

    def marker_matrices(s):
        wx[...] = matrix(s, CENTRE_ROWS, 64 * gx + centre_start, 0)
        high, low = split(matrix(s, 128, 128 * gy, 1))
        wy_high[...] = high
        wy_low[...] = low

    def sample(s):
        u = mom[0:3, pl.ds(centre_start, CENTRE_ROWS), :].reshape(3 * CENTRE_ROWS, 128)
        along = product(u, wy_high[...], wy_low[...], ((1,), (0,)))
        spread = wx[...]
        rows = [
            jnp.sum(along[c * CENTRE_ROWS : (c + 1) * CENTRE_ROWS] * spread, axis=0, keepdims=True)
            for c in range(3)
        ]
        sp[s, quarter] = jnp.concatenate(rows + [jnp.zeros((5, 256), jnp.float32)], axis=0)

    def pack_strips():
        packed = jnp.zeros((SIZE, 128), jnp.float32)
        for c in range(3):
            for b in range(CENTRE_ROWS // SIZE):
                value = mom[c, pl.ds(pl.multiple_of(centre_start + SIZE * b, 8), SIZE), :]
                first = 4 * (3 * c + b)
                value = pltpu.roll(value, first + 4 * (1 - gy), 1)
                packed = jnp.where((lanes >= first) & (lanes < first + 4), value, packed)
        strip_out[...] = packed

    def sample_full():
        u = mom[0:3, pl.ds(centre_start, CENTRE_ROWS), :].reshape(3 * CENTRE_ROWS, 128)
        beside = rows_in[...].reshape(24, 128)
        along = product(
            jnp.concatenate([u, beside], axis=0), wy_high[...], wy_low[...], ((1,), (0,))
        )
        spread = wx[...]
        spread_beside = matrix(0, 8, 64 * gx + 64 - 72 * flip, 0)
        wanted = jnp.where(gy == 0, lanes, 127 - lanes) < 4
        packed = strip_in[...]
        pieces = []
        for c in range(3):
            for b in range(CENTRE_ROWS // SIZE):
                shift = lax.rem(256 - 4 * (3 * c + b) - 4 * gy, 128)
                pieces.append(jnp.where(wanted, pltpu.roll(packed, shift, 1), 0.0))
        across = product(
            jnp.concatenate(pieces, axis=0), *split(matrix(0, 128, 128 * (1 - gy), 1)), ((1,), (0,))
        )
        rows = []
        for c in range(3):
            part = slice(c * CENTRE_ROWS, (c + 1) * CENTRE_ROWS)
            first = 3 * CENTRE_ROWS + 8 * c
            total = jnp.sum((along[part] + across[part]) * spread, axis=0, keepdims=True)
            total += jnp.sum(along[first : first + 8] * spread_beside, axis=0, keepdims=True)
            rows.append(total)
        full[...] = jnp.concatenate(rows, axis=0)

    def sampled(s):
        return (sp[s, 0] + sp[s, 1]) + (sp[s, 2] + sp[s, 3])

    def force(s):
        push = mk[10:13, :] - (full[...] if s == 0 else sampled(s)[0:3, :])
        spread = wx[...]
        weighted = jnp.concatenate([spread * push[c : c + 1, :] for c in range(3)], axis=0)
        body = product(weighted, wy_high[...], wy_low[...], ((1,), (1,)))
        fb[...] = body.reshape(3, CENTRE_ROWS, 128)

    for load in loads[:4]:
        load.wait()
    mk_own[...] = jnp.zeros((16, 128), jnp.float32)
    mk_own[0:2, 0:32] = cells[:, 0, :].astype(jnp.float32)
    mk_own[2:6, 0:32] = weights[0, :, 0, :]
    mk_own[6:10, 0:32] = weights[1, :, 0, :]
    mk_own[10:13, 0:32] = target[:, 0, :]
    mk_all[own] = pltpu.roll(mk_own[...], 32 * lax.rem(own, 4), 1)

    pl.semaphore_wait(barrier, len(neighbours))
    vouched = [neighbours[0], neighbours[1], neighbours[3]]
    for place in vouched:
        pl.semaphore_signal(vouch_sem, inc=1, device_id=place, device_id_type=MESH)

    for t in range(4):

        @pl.when(not_self(t))
        def _(t=t):
            marker_copy(t).start()

    for load in loads[4:]:
        load.wait()

    for s in range(STEPS):
        last = s == STEPS - 1
        if s > 0:
            for copy in [axial(s - 1, way, part) for way in range(2) for part in range(2)] + small(s - 1):
                copy.wait_recv()
            patch(pb[s - 1], er[s - 1], pp)

        @pl.when(centre)
        def _(s=s):
            if s == 1:
                for copy in strip_copies():
                    copy.wait_send()
            lax.fori_loop(OUTER_BLOCKS, BLOCKS, first_half(s), 0, unroll=True)
            if s == 0:
                pack_strips()
                for copy in strip_copies():
                    copy.start()
            else:
                sample(s)
                for copy in sample_copies(s):
                    copy.start()

        lax.fori_loop(0, OUTER_BLOCKS, whole_block(s), 0, unroll=True)
        for way in range(2):
            axial(s, way, 0).start()

        @pl.when(outer)
        def _(s=s):
            lax.fori_loop(OUTER_BLOCKS, BLOCKS, whole_block(s), 0, unroll=True)

        @pl.when(centre)
        def _(s=s):
            if s == 0:
                for d in range(1, 8):
                    marker_wait(lax.rem(own + d, 8))
                mk[:, 0:128] = (mk_all[0] + mk_all[1]) + (mk_all[2] + mk_all[3])
                mk[:, 128:256] = (mk_all[4] + mk_all[5]) + (mk_all[6] + mk_all[7])
                marker_matrices(s)
                for copy in strip_copies():
                    copy.wait_recv()
                sample_full()
            else:
                for d in range(1, 4):
                    sample_wait(s, lax.rem(quarter + d, 4))
            force(s)
            lax.fori_loop(OUTER_BLOCKS, BLOCKS, second_half(s), 0, unroll=True)

        if s == 0:
            pl.semaphore_wait(vouch_sem, len(vouched))
        for copy in small(s)[::-1]:
            copy.start()
        for way in range(2):
            axial(s, way, 1).start()

        if not last:

            @pl.when(centre)
            def _(s=s):
                marker_matrices(s + 1)

    for copy in [axial(STEPS - 1, way, part) for way in range(2) for part in range(2)] + small(STEPS - 1):
        copy.wait_recv()

    @pl.when(outer)
    def _():
        for q in range(4):
            sample_wait(STEPS - 1, q)

    total = sampled(STEPS - 1)
    half = jnp.where(own // 4 == 0, total[:, 0:128], total[:, 128:256])
    half = pltpu.roll(half, lax.rem(128 - 32 * lax.rem(own, 4), 128), 1)
    force_last[:, 0, :] = (target[:, 0, :] - half[0:3, 0:32]) * (1.0 / SPEED_SCALE)

    for t in range(4):

        @pl.when(not_self(t))
        def _(t=t):
            marker_copy(t).wait_send()

    for s in range(STEPS):
        for copy in [axial(s, way, part) for way in range(2) for part in range(2)] + small(s):
            copy.wait_send()

    @pl.when(centre)
    def _():
        for s in range(1, STEPS):
            for copy in sample_copies(s):
                copy.wait_send()


def finish(pb, zr, er, force, solid, res_pops, res_vel, res_force, pp, out_pops, out_vel, sem):
    patch(pb, er, pp)
    copies = []
    for rb in range(BLOCKS):
        rows = pl.ds(rb * SIZE, SIZE)
        f = streamed(pb, zr, er, pp, rb)
        for m in range(19):
            out_pops[m, 0, rows, :] = f[m]
        _, _, u = moments(f)
        fluid = solid[0, rows, :] == 0
        for c in range(3):
            out_vel[c, 0, rows, :] = jnp.where(fluid, u[c] * (1.0 / SPEED_SCALE), 0.0)
        for k, (src, dst) in enumerate([(out_pops, res_pops), (out_vel, res_vel)]):
            copy = pltpu.make_async_copy(
                src.at[:, :, rows, :], dst.at[:, :, rows, :], sem.at[2 * rb + k]
            )
            copy.start()
            copies.append(copy)
    copy = pltpu.make_async_copy(force, res_force, sem.at[2 * BLOCKS])
    copy.start()
    copies.append(copy)
    for copy in copies:
        copy.wait()


def body(populations, solid_mask, whirl_offsets, marker_cells, marker_weights, pipe_velocity):
    f32 = jnp.float32
    vmem = pl.BlockSpec(memory_space=pltpu.VMEM)
    hbm = pl.BlockSpec(memory_space=pltpu.HBM)
    pb, zr, er = (9, 80, 128), (2, 5, 80, 128), (5, SIZE, 128)
    arrived = pl.pallas_call(
        functools.partial(kernel, lax.axis_size("gz")),
        out_shape=[pltpu.VMEM(shape, f32) for shape in (pb, zr, er, pipe_velocity.shape)],
        in_specs=[hbm] * 6,
        out_specs=[vmem] * 4,
        scratch_shapes=[
            pltpu.VMEM((STEPS - 1,) + pb, f32),
            pltpu.VMEM((STEPS, 2, 5, 64, 128), f32),
            pltpu.VMEM((STEPS - 1,) + zr, f32),
            pltpu.VMEM((STEPS, SIZE, 128), f32),
            pltpu.VMEM((STEPS - 1,) + er, f32),
            pltpu.VMEM((4, 80, 128), f32),
            pltpu.VMEM((19, 64, 128), f32),
            pltpu.VMEM((5, 64, 128), f32),
            pltpu.VMEM((3, CENTRE_ROWS, 128), f32),
            pltpu.VMEM((16, 128), f32),
            pltpu.VMEM((8, 16, 128), f32),
            pltpu.VMEM((16, 256), f32),
            pltpu.VMEM((STEPS, 4, 8, 256), f32),
            pltpu.VMEM((CENTRE_ROWS, 256), f32),
            pltpu.VMEM((128, 256), jnp.bfloat16),
            pltpu.VMEM((128, 256), jnp.bfloat16),
            pltpu.SemaphoreType.DMA((STEPS, N_MESSAGES)),
            pltpu.SemaphoreType.DMA((STEPS, N_MESSAGES)),
            pltpu.SemaphoreType.DMA((4,)),
            pltpu.SemaphoreType.DMA((8,)),
            pltpu.VMEM(populations.shape, f32),
            pltpu.VMEM(solid_mask.shape, jnp.int32),
            pltpu.SMEM(whirl_offsets.shape[::-1], jnp.int32),
            pltpu.VMEM(marker_cells.shape, jnp.int32),
            pltpu.VMEM(marker_weights.shape, f32),
            pltpu.VMEM(pipe_velocity.shape, f32),
            pltpu.VMEM((SIZE, 128), f32),
            pltpu.VMEM((SIZE, 128), f32),
            pltpu.VMEM((3, 8, 128), f32),
            pltpu.VMEM((3, 256), f32),
            pltpu.SemaphoreType.DMA((6,)),
            pltpu.SemaphoreType.REGULAR,
        ],
        compiler_params=pltpu.CompilerParams(
            collective_id=0, has_side_effects=True, vmem_limit_bytes=60 * 1024 * 1024
        ),
        cost_estimate=pl.CostEstimate(flops=40_000_000, bytes_accessed=2_000_000, transcendentals=0),
    )(populations, solid_mask, whirl_offsets.T, marker_cells, marker_weights, pipe_velocity)
    shapes = (populations.shape, (3,) + solid_mask.shape, pipe_velocity.shape)
    return pl.pallas_call(
        finish,
        out_shape=[jax.ShapeDtypeStruct(shape, f32) for shape in shapes],
        in_specs=[vmem] * 5,
        out_specs=[hbm] * 3,
        scratch_shapes=[pltpu.VMEM((4, 80, 128), f32)]
        + [pltpu.VMEM(shape, f32) for shape in shapes[:2]]
        + [pltpu.SemaphoreType.DMA((2 * BLOCKS + 1,))],
        compiler_params=pltpu.CompilerParams(vmem_limit_bytes=24 * 1024 * 1024),
        cost_estimate=pl.CostEstimate(flops=2_000_000, bytes_accessed=2_000_000, transcendentals=0),
    )(*arrived, solid_mask)


def solution(mesh):
    in_specs = (
        P(None, "gz", "gx", "gy"),
        P("gz", "gx", "gy"),
        P(),
        P(None, "gz", ("gx", "gy")),
        P(None, None, "gz", ("gx", "gy")),
        P(None, "gz", ("gx", "gy")),
    )
    out_specs = (P(None, "gz", "gx", "gy"), P(None, "gz", "gx", "gy"), P(None, "gz", ("gx", "gy")))
    return jax.shard_map(body, mesh=mesh, in_specs=in_specs, out_specs=out_specs, check_vma=False)
```

```python
import functools

import jax
import jax.numpy as jnp
from jax import lax
from jax.experimental import pallas as pl
from jax.experimental.pallas import tpu as pltpu
from jax.sharding import PartitionSpec as P

MESH = pl.DeviceIdType.MESH
STEPS = 3
RELAX_TIME = 0.8
SPEED_SCALE = 0.05

VELOCITIES = [
    (0, 0, 0),
    (1, 0, 0),
    (-1, 0, 0),
    (0, 1, 0),
    (0, -1, 0),
    (0, 0, 1),
    (0, 0, -1),
    (1, 1, 0),
    (-1, -1, 0),
    (1, -1, 0),
    (-1, 1, 0),
    (1, 0, 1),
    (-1, 0, -1),
    (1, 0, -1),
    (-1, 0, 1),
    (0, 1, 1),
    (0, -1, -1),
    (0, 1, -1),
    (0, -1, 1),
]
INDEX = {vector: member for member, vector in enumerate(VELOCITIES)}
INPLANE = [
    (0, 0, 0),
    (0, 0, 1),
    (0, 0, -1),
    (0, 1, 0),
    (0, 1, 1),
    (0, 1, -1),
    (0, -1, 0),
    (0, -1, 1),
    (0, -1, -1),
]
AXIAL = [
    [(1, 0, 0), (1, 0, 1), (1, 0, -1), (1, 1, 0), (1, -1, 0)],
    [(-1, 0, 0), (-1, 0, 1), (-1, 0, -1), (-1, 1, 0), (-1, -1, 0)],
]
EDGES = [
    (0, 0, 1),
    (0, 0, -1),
    (0, 1, 1),
    (0, 1, -1),
    (0, -1, 1),
    (0, -1, -1),
    (1, 0, 1),
    (1, 0, -1),
    (-1, 0, 1),
    (-1, 0, -1),
]
DIAGONAL = [(0, 1, 1), (0, 1, -1), (0, -1, 1), (0, -1, -1)]

SIZE = 8
BLOCKS = 8
OUTER_BLOCKS = 3
OUTER_ROWS = SIZE * OUTER_BLOCKS
CENTRE_BLOCKS = BLOCKS - OUTER_BLOCKS
CENTRE_ROWS = SIZE * CENTRE_BLOCKS
SPAN = 128 // BLOCKS
N_AXIAL = 0
N_AXIAL_ROW = 4
N_ROW = 8
N_EDGE = 10
N_SAMPLE = 15
N_STRIP = 22
N_MESSAGES = 24


def tree_sum(values):
    while len(values) > 1:
        pairs = [values[i] + values[i + 1] for i in range(0, len(values) - 1, 2)]
        if len(values) % 2:
            pairs.append(values[-1])
        values = pairs
    return values[0]


def moments(f):
    density = tree_sum(f)
    inverse = 1.0 / density
    components = []
    for column in range(3):
        ahead = tree_sum([f[m] for m in range(19) if VELOCITIES[m][column] == 1])
        back = tree_sum([f[m] for m in range(19) if VELOCITIES[m][column] == -1])
        components.append((ahead - back) * inverse)
    return density, inverse, components


def dot(vector, u):
    total = None
    for c, x in zip(vector, u):
        if c == 0:
            continue
        if total is None:
            total = x if c == 1 else -x
        else:
            total = total + x if c == 1 else total - x
    return total


def collide(f, density, u, fluid):
    base = 1.0 - 1.5 * (u[0] * u[0] + u[1] * u[1] + u[2] * u[2])
    keep = 1.0 - 1.0 / RELAX_TIME
    scaled = density * (1.0 / RELAX_TIME)
    heavy = scaled * (1.0 / 18.0)
    light = scaled * (1.0 / 36.0)
    post = [None] * 19
    post[0] = jnp.where(fluid, scaled * (1.0 / 3.0) * base + keep * f[0], f[0])
    for m in range(1, 19, 2):
        weight = heavy if m < 7 else light
        projected = dot(VELOCITIES[m], u)
        even = weight * (base + 4.5 * (projected * projected))
        odd = (3.0 * weight) * projected
        post[m] = jnp.where(fluid, (even + odd) + keep * f[m], f[m + 1])
        post[m + 1] = jnp.where(fluid, (even - odd) + keep * f[m + 1], f[m])
    return post


def split(x):
    high = x.astype(jnp.bfloat16)
    low = (x - high.astype(jnp.float32)).astype(jnp.bfloat16)
    return high, low


def product(x, w_high, w_low, dims):
    high, low = split(x)
    one = functools.partial(
        lax.dot_general, dimension_numbers=(dims, ((), ())), preferred_element_type=jnp.float32
    )
    return one(high, w_high) + (one(low, w_high) + one(high, w_low))


def edge(value, packed, vector):
    j = EDGES.index(vector)
    lane = lax.broadcasted_iota(jnp.int32, value.shape, 1)
    if vector[2] == 1:
        there = packed if j == 0 else pltpu.roll(packed, 128 - j, 1)
        return jnp.where(lane == 0, there, value)
    return jnp.where(lane == 127, pltpu.roll(packed, 127 - j, 1), value)


def unpacked(packed, rb):
    return pltpu.roll(packed, lax.rem(128 - SPAN * rb, 128), 1)


def patch(pb, er, pp):
    def block(rb, carry):
        row = pl.multiple_of(rb * SIZE + 8, 8)
        packed = unpacked(er[0], rb)
        for k, vector in enumerate(DIAGONAL):
            value = pb[INPLANE.index(vector), pl.ds(row, SIZE), :]
            pp[k, pl.ds(row, SIZE), :] = edge(value, packed, vector)
        return carry

    lax.fori_loop(0, BLOCKS, block, 0, unroll=True)
    before = pltpu.roll(er[1, SIZE - 8 :, :], SPAN, 1)
    after = er[2, 0:8, :]
    for k, vector in enumerate(DIAGONAL):
        packed, row = (before, 0) if vector[1] == 1 else (after, 72)
        value = pb[INPLANE.index(vector), pl.ds(row, 8), :]
        pp[k, pl.ds(row, 8), :] = edge(value, packed, vector)


def streamed(pb, zr, er, pp, rb):
    row = pl.multiple_of(rb * SIZE, 8)
    packed = {0: unpacked(er[0], rb), 1: unpacked(er[3], rb), -1: unpacked(er[4], rb)}
    f = []
    for vector in VELOCITIES:
        rows = pl.ds(row + (8 - vector[1]), SIZE)
        if vector in DIAGONAL:
            f.append(pp[DIAGONAL.index(vector), rows, :])
            continue
        if vector[0] == 0:
            value = pb[INPLANE.index(vector), rows, :]
        else:
            way = 0 if vector[0] == 1 else 1
            value = zr[way, AXIAL[way].index(vector), rows, :]
        if vector[2] != 0:
            value = edge(value, packed[vector[0]], vector)
        f.append(value)
    return f


def kernel(
    gz_size,
    pops_in,
    solid_in,
    whirl_in,
    cells_in,
    weights_in,
    target_in,
    pb_last,
    zr_last,
    er_last,
    force_last,
    pb_early,
    zs,
    zr_early,
    es,
    er_early,
    pp,
    st,
    mom,
    fb,
    mk_own,
    mk_all,
    mk,
    sp,
    wx,
    wy_high,
    wy_low,
    send_sem,
    recv_sem,
    mk_send,
    mk_recv,
    pops,
    solid,
    whirl,
    cells,
    weights,
    target,
    strip_out,
    strip_in,
    rows_in,
    full,
    load_sem,
    vouch_sem,
):
    loads = [
        pltpu.make_async_copy(src, dst, load_sem.at[k])
        for k, (src, dst) in enumerate(
            [
                (cells_in, cells),
                (weights_in, weights),
                (target_in, target),
                (whirl_in, whirl),
                (pops_in, pops),
                (solid_in, solid),
            ]
        )
    ]
    for load in loads:
        load.start()
    pb = [pb_early.at[s] for s in range(STEPS - 1)] + [pb_last]
    zr = [zr_early.at[s] for s in range(STEPS - 1)] + [zr_last]
    er = [er_early.at[s] for s in range(STEPS - 1)] + [er_last]
    gz = lax.axis_index("gz")
    gx = lax.axis_index("gx")
    gy = lax.axis_index("gy")
    z_next, z_prev = lax.rem(gz + 1, gz_size), lax.rem(gz + gz_size - 1, gz_size)
    x_next, x_prev, x_far = lax.rem(gx + 1, 4), lax.rem(gx + 3, 4), lax.rem(gx + 2, 4)
    y_other = 1 - gy
    flip = gx // 2
    is_centre = lax.rem((gx + 1) // 2, 2)
    centre = is_centre == 1
    outer = is_centre == 0
    quarter = lax.rem(2 * gx + gy + 2, 4)
    own = 2 * gx + gy
    outer_start = pl.multiple_of(CENTRE_ROWS * flip, 8)
    centre_start = pl.multiple_of(OUTER_ROWS * (1 - flip), 8)

    barrier = pltpu.get_barrier_semaphore()
    neighbours = [
        {"gz": gz, "gx": x_next, "gy": gy},
        {"gz": gz, "gx": x_prev, "gy": gy},
        {"gz": gz, "gx": x_far, "gy": gy},
        {"gz": gz, "gx": gx, "gy": y_other},
        {"gz": gz, "gx": x_next, "gy": y_other},
        {"gz": gz, "gx": x_prev, "gy": y_other},
        {"gz": gz, "gx": x_far, "gy": y_other},
    ]
    for z in (z_next, z_prev):
        neighbours.append({"gz": z, "gx": gx, "gy": gy})
    for place in neighbours:
        pl.semaphore_signal(barrier, inc=1, device_id=place, device_id_type=MESH)

    lanes = lax.broadcasted_iota(jnp.int32, (SIZE, 128), 1)
    lane_block = lanes // SPAN

    def block_of(b):
        return b + flip * (BLOCKS - 1 - 2 * b)

    def remote(src, dst, s, n, place, n_recv=None):
        return pltpu.make_async_remote_copy(
            src_ref=src,
            dst_ref=dst,
            send_sem=send_sem.at[s, n],
            recv_sem=recv_sem.at[s, n if n_recv is None else n_recv],
            device_id=place,
            device_id_type=MESH,
        )

    def axial(s, way, part):
        start, size = ((outer_start, OUTER_ROWS), (centre_start, CENTRE_ROWS))[part]
        return remote(
            zs.at[s, way, :, pl.ds(start, size), :],
            zr[s].at[way, :, pl.ds(pl.multiple_of(start + 8, 8), size), :],
            s,
            N_AXIAL + 2 * way + part,
            {"gz": (z_next, z_prev)[way], "gx": gx, "gy": gy},
        )

    def small(s):
        copies = []
        for way in range(2):
            z = (z_next, z_prev)[way]
            copies.append(
                remote(
                    zs.at[s, way, 3, pl.ds(56, 8), :],
                    zr[s].at[way, 3, pl.ds(0, 8), :],
                    s,
                    N_AXIAL_ROW + 2 * way,
                    {"gz": z, "gx": x_next, "gy": gy},
                )
            )
            copies.append(
                remote(
                    zs.at[s, way, 4, pl.ds(0, 8), :],
                    zr[s].at[way, 4, pl.ds(72, 8), :],
                    s,
                    N_AXIAL_ROW + 2 * way + 1,
                    {"gz": z, "gx": x_prev, "gy": gy},
                )
            )
        copies.append(
            remote(
                pb[s].at[pl.ds(3, 3), pl.ds(64, 8), :],
                pb[s].at[pl.ds(3, 3), pl.ds(0, 8), :],
                s,
                N_ROW,
                {"gz": gz, "gx": x_next, "gy": gy},
            )
        )
        copies.append(
            remote(
                pb[s].at[pl.ds(6, 3), pl.ds(8, 8), :],
                pb[s].at[pl.ds(6, 3), pl.ds(72, 8), :],
                s,
                N_ROW + 1,
                {"gz": gz, "gx": x_prev, "gy": gy},
            )
        )
        places = [
            {"gz": gz, "gx": gx, "gy": y_other},
            {"gz": gz, "gx": x_next, "gy": y_other},
            {"gz": gz, "gx": x_prev, "gy": y_other},
            {"gz": z_next, "gx": gx, "gy": y_other},
            {"gz": z_prev, "gx": gx, "gy": y_other},
        ]
        for k, place in enumerate(places):
            copies.append(remote(es.at[s], er[s].at[k], s, N_EDGE + k, place))
        return copies

    def sample_copies(s):
        pair = 3 - gx
        places = [(gx, y_other), (pair, gy), (pair, y_other)]
        if s == STEPS - 1:
            places += [(0, gy), (0, y_other), (3, gy), (3, y_other)]
        return [
            remote(
                sp.at[s, quarter],
                sp.at[s, quarter],
                s,
                N_SAMPLE + d,
                {"gz": gz, "gx": x, "gy": y},
                N_SAMPLE + quarter,
            )
            for d, (x, y) in enumerate(places)
        ]

    def sample_wait(s, q):
        remote(sp.at[s, q], sp.at[s, q], s, N_SAMPLE, neighbours[0], N_SAMPLE + q).wait_recv()

    def strip_copies():
        edge_rows = pl.ds(pl.multiple_of(56 - 56 * flip, 8), 8)
        return [
            remote(
                mom.at[pl.ds(0, 3), edge_rows, :],
                rows_in,
                0,
                N_STRIP,
                {"gz": gz, "gx": 3 - gx, "gy": gy},
            ),
            remote(strip_out, strip_in, 0, N_STRIP + 1, {"gz": gz, "gx": gx, "gy": y_other}),
        ]

    def centre_place(t):
        return {"gz": gz, "gx": 1 + t // 2, "gy": t % 2}

    def marker_copy(t):
        return pltpu.make_async_remote_copy(
            src_ref=mk_all.at[own],
            dst_ref=mk_all.at[own],
            send_sem=mk_send.at[t],
            recv_sem=mk_recv.at[own],
            device_id=centre_place(t),
            device_id_type=MESH,
        )

    def marker_wait(j):
        pltpu.make_async_remote_copy(
            src_ref=mk_all.at[j],
            dst_ref=mk_all.at[j],
            send_sem=mk_send.at[0],
            recv_sem=mk_recv.at[j],
            device_id=neighbours[0],
            device_id_type=MESH,
        ).wait_recv()

    def not_self(t):
        return jnp.logical_or(gx != 1 + t // 2, gy != t % 2)

    def gather(s, rb):
        if s == 0:
            row = pl.multiple_of(rb * SIZE, 8)
            return [pops[m, 0, pl.ds(row, SIZE), :] for m in range(19)]
        return streamed(pb[s - 1], zr[s - 1], er[s - 1], pp, rb)

    def store_post(s, rb, post):
        row = pl.multiple_of(rb * SIZE, 8)
        for vector in VELOCITIES:
            value = post[INDEX[vector]]
            if vector[2] != 0:
                value = pltpu.roll(value, 1 if vector[2] == 1 else 127, 1)
            if vector[0] == 0:
                pb[s][INPLANE.index(vector), pl.ds(pl.multiple_of(row + 8, 8), SIZE), :] = value
            else:
                way = 0 if vector[0] == 1 else 1
                zs[s, way, AXIAL[way].index(vector), pl.ds(row, SIZE), :] = value
        packed = post[INDEX[EDGES[0]]]
        packed = pltpu.roll(packed, 1, 1)
        for j, vector in enumerate(EDGES):
            if j == 0:
                continue
            shift = j + 1 if vector[2] == 1 else j
            packed = jnp.where(lanes == j, pltpu.roll(post[INDEX[vector]], shift, 1), packed)
        es[s] = jnp.where(lane_block == rb, pltpu.roll(packed, SPAN * rb, 1), es[s])

    def fluid_of(rb):
        return solid[0, pl.ds(pl.multiple_of(rb * SIZE, 8), SIZE), :] == 0

    def whole_block(s):
        def block(b, carry):
            rb = block_of(b)
            f = gather(s, rb)
            density, _, u = moments(f)
            store_post(s, rb, collide(f, density, u, fluid_of(rb)))
            return carry

        return block

    def first_half(s):
        def block(b, carry):
            rb = block_of(b)
            row = pl.multiple_of(rb * SIZE, 8)
            f = gather(s, rb)
            density, inverse, u = moments(f)
            if s > 0:
                for m in range(19):
                    st[m, pl.ds(row, SIZE), :] = f[m]
            for c, value in enumerate([*u, density, inverse]):
                mom[c, pl.ds(row, SIZE), :] = value
            return carry

        return block

    def second_half(s):
        def block(b, carry):
            rb = block_of(b)
            row = pl.multiple_of(rb * SIZE, 8)
            if s == 0:
                f = [pops[m, 0, pl.ds(row, SIZE), :] for m in range(19)]
            else:
                f = [st[m, pl.ds(row, SIZE), :] for m in range(19)]
            density = mom[3, pl.ds(row, SIZE), :]
            scale = RELAX_TIME * mom[4, pl.ds(row, SIZE), :]
            near = pl.multiple_of(row - centre_start, 8)
            u = [mom[c, pl.ds(row, SIZE), :] + scale * fb[c, pl.ds(near, SIZE), :] for c in range(3)]
            store_post(s, rb, collide(f, density, u, fluid_of(rb)))
            return carry

        return block

    def matrix(s, size, first, dim):
        base = mk[dim : dim + 1, :] + (127 + whirl[dim, s]).astype(jnp.float32)
        place = lax.broadcasted_iota(jnp.int32, (size, 256), 0) + first
        distance = place.astype(jnp.float32) - base
        result = jnp.zeros((size, 256), jnp.float32)
        for a in range(4):
            row = 2 + 4 * dim + a
            result = jnp.where(distance == float(a), mk[row : row + 1, :], result)
        return result

    def marker_matrices(s):
        wx[...] = matrix(s, CENTRE_ROWS, 64 * gx + centre_start, 0)
        high, low = split(matrix(s, 128, 128 * gy, 1))
        wy_high[...] = high
        wy_low[...] = low

    def sample(s):
        u = mom[0:3, pl.ds(centre_start, CENTRE_ROWS), :].reshape(3 * CENTRE_ROWS, 128)
        along = product(u, wy_high[...], wy_low[...], ((1,), (0,)))
        spread = wx[...]
        rows = [
            jnp.sum(along[c * CENTRE_ROWS : (c + 1) * CENTRE_ROWS] * spread, axis=0, keepdims=True)
            for c in range(3)
        ]
        sp[s, quarter] = jnp.concatenate(rows + [jnp.zeros((5, 256), jnp.float32)], axis=0)

    def pack_strips():
        packed = jnp.zeros((SIZE, 128), jnp.float32)
        for c in range(3):
            for b in range(CENTRE_BLOCKS):
                value = mom[c, pl.ds(pl.multiple_of(centre_start + SIZE * b, 8), SIZE), :]
                first = 4 * (CENTRE_BLOCKS * c + b)
                value = pltpu.roll(value, first + 4 * (1 - gy), 1)
                packed = jnp.where((lanes >= first) & (lanes < first + 4), value, packed)
        strip_out[...] = packed

    def sample_full():
        u = mom[0:3, pl.ds(centre_start, CENTRE_ROWS), :].reshape(3 * CENTRE_ROWS, 128)
        beside = rows_in[...].reshape(24, 128)
        along = product(
            jnp.concatenate([u, beside], axis=0), wy_high[...], wy_low[...], ((1,), (0,))
        )
        spread = wx[...]
        spread_beside = matrix(0, 8, 64 * gx + 64 - 72 * flip, 0)
        wanted = jnp.where(gy == 0, lanes, 127 - lanes) < 4
        packed = strip_in[...]
        pieces = []
        for c in range(3):
            for b in range(CENTRE_BLOCKS):
                shift = lax.rem(256 - 4 * (CENTRE_BLOCKS * c + b) - 4 * gy, 128)
                pieces.append(jnp.where(wanted, pltpu.roll(packed, shift, 1), 0.0))
        across = product(
            jnp.concatenate(pieces, axis=0), *split(matrix(0, 128, 128 * (1 - gy), 1)), ((1,), (0,))
        )
        rows = []
        for c in range(3):
            part = slice(c * CENTRE_ROWS, (c + 1) * CENTRE_ROWS)
            first = 3 * CENTRE_ROWS + 8 * c
            total = jnp.sum((along[part] + across[part]) * spread, axis=0, keepdims=True)
            total += jnp.sum(along[first : first + 8] * spread_beside, axis=0, keepdims=True)
            rows.append(total)
        full[...] = jnp.concatenate(rows, axis=0)

    def sampled(s):
        return (sp[s, 0] + sp[s, 1]) + (sp[s, 2] + sp[s, 3])

    def force(s):
        push = mk[10:13, :] - (full[...] if s == 0 else sampled(s)[0:3, :])
        spread = wx[...]
        weighted = jnp.concatenate([spread * push[c : c + 1, :] for c in range(3)], axis=0)
        body = product(weighted, wy_high[...], wy_low[...], ((1,), (1,)))
        fb[...] = body.reshape(3, CENTRE_ROWS, 128)

    for load in loads[:4]:
        load.wait()
    mk_own[...] = jnp.zeros((16, 128), jnp.float32)
    mk_own[0:2, 0:32] = cells[:, 0, :].astype(jnp.float32)
    mk_own[2:6, 0:32] = weights[0, :, 0, :]
    mk_own[6:10, 0:32] = weights[1, :, 0, :]
    mk_own[10:13, 0:32] = target[:, 0, :]
    mk_all[own] = pltpu.roll(mk_own[...], 32 * lax.rem(own, 4), 1)

    pl.semaphore_wait(barrier, len(neighbours))
    vouched = [neighbours[0], neighbours[1], neighbours[3]]
    for place in vouched:
        pl.semaphore_signal(vouch_sem, inc=1, device_id=place, device_id_type=MESH)

    for t in range(4):

        @pl.when(not_self(t))
        def _(t=t):
            marker_copy(t).start()

    for load in loads[4:]:
        load.wait()

    for s in range(STEPS):
        last = s == STEPS - 1
        if s > 0:
            for copy in [axial(s - 1, way, part) for way in range(2) for part in range(2)] + small(s - 1):
                copy.wait_recv()
            patch(pb[s - 1], er[s - 1], pp)

        @pl.when(centre)
        def _(s=s):
            if s == 1:
                for copy in strip_copies():
                    copy.wait_send()
            lax.fori_loop(OUTER_BLOCKS, BLOCKS, first_half(s), 0, unroll=True)
            if s == 0:
                pack_strips()
                for copy in strip_copies():
                    copy.start()
            else:
                sample(s)
                for copy in sample_copies(s):
                    copy.start()

        lax.fori_loop(0, OUTER_BLOCKS, whole_block(s), 0, unroll=True)
        for way in range(2):
            axial(s, way, 0).start()

        @pl.when(outer)
        def _(s=s):
            lax.fori_loop(OUTER_BLOCKS, BLOCKS, whole_block(s), 0, unroll=True)

        @pl.when(centre)
        def _(s=s):
            if s == 0:
                for d in range(1, 8):
                    marker_wait(lax.rem(own + d, 8))
                mk[:, 0:128] = (mk_all[0] + mk_all[1]) + (mk_all[2] + mk_all[3])
                mk[:, 128:256] = (mk_all[4] + mk_all[5]) + (mk_all[6] + mk_all[7])
                marker_matrices(s)
                for copy in strip_copies():
                    copy.wait_recv()
                sample_full()
            else:
                for d in range(1, 4):
                    sample_wait(s, lax.rem(quarter + d, 4))
            force(s)
            lax.fori_loop(OUTER_BLOCKS, BLOCKS, second_half(s), 0, unroll=True)

        if s == 0:
            pl.semaphore_wait(vouch_sem, len(vouched))
        for copy in small(s)[::-1]:
            copy.start()
        for way in range(2):
            axial(s, way, 1).start()

        if not last:

            @pl.when(centre)
            def _(s=s):
                marker_matrices(s + 1)

    @pl.when(outer)
    def _():
        for q in range(4):
            sample_wait(STEPS - 1, q)

    total = sampled(STEPS - 1)
    half = jnp.where(own // 4 == 0, total[:, 0:128], total[:, 128:256])
    half = pltpu.roll(half, lax.rem(128 - 32 * lax.rem(own, 4), 128), 1)
    force_last[:, 0, :] = (target[:, 0, :] - half[0:3, 0:32]) * (1.0 / SPEED_SCALE)

    for t in range(4):

        @pl.when(not_self(t))
        def _(t=t):
            marker_copy(t).wait_send()

    @pl.when(centre)
    def _():
        for s in range(1, STEPS):
            for copy in sample_copies(s):
                copy.wait_send()

    for s in range(STEPS):
        for copy in small(s) + [axial(s, way, part) for part in range(2) for way in range(2)]:
            copy.wait_send()

    for copy in small(STEPS - 1)[::-1] + [
        axial(STEPS - 1, way, part) for part in range(2) for way in range(2)
    ]:
        copy.wait_recv()


def finish(pb, zr, er, force, solid, res_pops, res_vel, res_force, pp, out_pops, out_vel, sem):
    patch(pb, er, pp)
    copies = []
    for rb in range(BLOCKS):
        rows = pl.ds(rb * SIZE, SIZE)
        f = streamed(pb, zr, er, pp, rb)
        for m in range(19):
            out_pops[m, 0, rows, :] = f[m]
        _, _, u = moments(f)
        fluid = solid[0, rows, :] == 0
        for c in range(3):
            out_vel[c, 0, rows, :] = jnp.where(fluid, u[c] * (1.0 / SPEED_SCALE), 0.0)
        for k, (src, dst) in enumerate([(out_pops, res_pops), (out_vel, res_vel)]):
            copy = pltpu.make_async_copy(
                src.at[:, :, rows, :], dst.at[:, :, rows, :], sem.at[2 * rb + k]
            )
            copy.start()
            copies.append(copy)
    copy = pltpu.make_async_copy(force, res_force, sem.at[2 * BLOCKS])
    copy.start()
    copies.append(copy)
    for copy in copies:
        copy.wait()


def body(populations, solid_mask, whirl_offsets, marker_cells, marker_weights, pipe_velocity):
    f32 = jnp.float32
    vmem = pl.BlockSpec(memory_space=pltpu.VMEM)
    hbm = pl.BlockSpec(memory_space=pltpu.HBM)
    pb, zr, er = (9, 80, 128), (2, 5, 80, 128), (5, SIZE, 128)
    arrived = pl.pallas_call(
        functools.partial(kernel, lax.axis_size("gz")),
        out_shape=[pltpu.VMEM(shape, f32) for shape in (pb, zr, er, pipe_velocity.shape)],
        in_specs=[hbm] * 6,
        out_specs=[vmem] * 4,
        scratch_shapes=[
            pltpu.VMEM((STEPS - 1,) + pb, f32),
            pltpu.VMEM((STEPS, 2, 5, 64, 128), f32),
            pltpu.VMEM((STEPS - 1,) + zr, f32),
            pltpu.VMEM((STEPS, SIZE, 128), f32),
            pltpu.VMEM((STEPS - 1,) + er, f32),
            pltpu.VMEM((4, 80, 128), f32),
            pltpu.VMEM((19, 64, 128), f32),
            pltpu.VMEM((5, 64, 128), f32),
            pltpu.VMEM((3, CENTRE_ROWS, 128), f32),
            pltpu.VMEM((16, 128), f32),
            pltpu.VMEM((8, 16, 128), f32),
            pltpu.VMEM((16, 256), f32),
            pltpu.VMEM((STEPS, 4, 8, 256), f32),
            pltpu.VMEM((CENTRE_ROWS, 256), f32),
            pltpu.VMEM((128, 256), jnp.bfloat16),
            pltpu.VMEM((128, 256), jnp.bfloat16),
            pltpu.SemaphoreType.DMA((STEPS, N_MESSAGES)),
            pltpu.SemaphoreType.DMA((STEPS, N_MESSAGES)),
            pltpu.SemaphoreType.DMA((4,)),
            pltpu.SemaphoreType.DMA((8,)),
            pltpu.VMEM(populations.shape, f32),
            pltpu.VMEM(solid_mask.shape, jnp.int32),
            pltpu.SMEM(whirl_offsets.shape[::-1], jnp.int32),
            pltpu.VMEM(marker_cells.shape, jnp.int32),
            pltpu.VMEM(marker_weights.shape, f32),
            pltpu.VMEM(pipe_velocity.shape, f32),
            pltpu.VMEM((SIZE, 128), f32),
            pltpu.VMEM((SIZE, 128), f32),
            pltpu.VMEM((3, 8, 128), f32),
            pltpu.VMEM((3, 256), f32),
            pltpu.SemaphoreType.DMA((6,)),
            pltpu.SemaphoreType.REGULAR,
        ],
        compiler_params=pltpu.CompilerParams(
            collective_id=0, has_side_effects=True, vmem_limit_bytes=60 * 1024 * 1024
        ),
        cost_estimate=pl.CostEstimate(flops=40_000_000, bytes_accessed=2_000_000, transcendentals=0),
    )(populations, solid_mask, whirl_offsets.T, marker_cells, marker_weights, pipe_velocity)
    shapes = (populations.shape, (3,) + solid_mask.shape, pipe_velocity.shape)
    return pl.pallas_call(
        finish,
        out_shape=[jax.ShapeDtypeStruct(shape, f32) for shape in shapes],
        in_specs=[vmem] * 5,
        out_specs=[hbm] * 3,
        scratch_shapes=[pltpu.VMEM((4, 80, 128), f32)]
        + [pltpu.VMEM(shape, f32) for shape in shapes[:2]]
        + [pltpu.SemaphoreType.DMA((2 * BLOCKS + 1,))],
        compiler_params=pltpu.CompilerParams(vmem_limit_bytes=24 * 1024 * 1024),
        cost_estimate=pl.CostEstimate(flops=2_000_000, bytes_accessed=2_000_000, transcendentals=0),
    )(*arrived, solid_mask)


def solution(mesh):
    in_specs = (
        P(None, "gz", "gx", "gy"),
        P("gz", "gx", "gy"),
        P(),
        P(None, "gz", ("gx", "gy")),
        P(None, None, "gz", ("gx", "gy")),
        P(None, "gz", ("gx", "gy")),
    )
    out_specs = (P(None, "gz", "gx", "gy"), P(None, "gz", "gx", "gy"), P(None, "gz", ("gx", "gy")))
    return jax.shard_map(body, mesh=mesh, in_specs=in_specs, out_specs=out_specs, check_vma=False)
```

```python
import functools

import jax
import jax.numpy as jnp
from jax import lax
from jax.experimental import pallas as pl
from jax.experimental.pallas import tpu as pltpu
from jax.sharding import PartitionSpec as P

MESH = pl.DeviceIdType.MESH
STEPS = 3
RELAX_TIME = 0.8
SPEED_SCALE = 0.05

VELOCITIES = [
    (0, 0, 0),
    (1, 0, 0),
    (-1, 0, 0),
    (0, 1, 0),
    (0, -1, 0),
    (0, 0, 1),
    (0, 0, -1),
    (1, 1, 0),
    (-1, -1, 0),
    (1, -1, 0),
    (-1, 1, 0),
    (1, 0, 1),
    (-1, 0, -1),
    (1, 0, -1),
    (-1, 0, 1),
    (0, 1, 1),
    (0, -1, -1),
    (0, 1, -1),
    (0, -1, 1),
]
INDEX = {vector: member for member, vector in enumerate(VELOCITIES)}
INPLANE = [
    (0, 0, 0),
    (0, 0, 1),
    (0, 0, -1),
    (0, 1, 0),
    (0, 1, 1),
    (0, 1, -1),
    (0, -1, 0),
    (0, -1, 1),
    (0, -1, -1),
]
AXIAL = [
    [(1, 0, 0), (1, 0, 1), (1, 0, -1), (1, 1, 0), (1, -1, 0)],
    [(-1, 0, 0), (-1, 0, 1), (-1, 0, -1), (-1, 1, 0), (-1, -1, 0)],
]
EDGES = [
    (0, 0, 1),
    (0, 0, -1),
    (0, 1, 1),
    (0, 1, -1),
    (0, -1, 1),
    (0, -1, -1),
    (1, 0, 1),
    (1, 0, -1),
    (-1, 0, 1),
    (-1, 0, -1),
]
DIAGONAL = [(0, 1, 1), (0, 1, -1), (0, -1, 1), (0, -1, -1)]

SIZE = 8
BLOCKS = 8
OUTER_BLOCKS = 3
OUTER_ROWS = SIZE * OUTER_BLOCKS
CENTRE_BLOCKS = BLOCKS - OUTER_BLOCKS
CENTRE_ROWS = SIZE * CENTRE_BLOCKS
SPAN = 128 // BLOCKS
N_AXIAL = 0
N_AXIAL_ROW = 4
N_ROW = 8
N_EDGE = 10
N_SAMPLE = 15
N_STRIP = 22
N_MESSAGES = 24


def tree_sum(values):
    while len(values) > 1:
        pairs = [values[i] + values[i + 1] for i in range(0, len(values) - 1, 2)]
        if len(values) % 2:
            pairs.append(values[-1])
        values = pairs
    return values[0]


def moments(f):
    density = tree_sum(f)
    inverse = 1.0 / density
    components = []
    for column in range(3):
        ahead = tree_sum([f[m] for m in range(19) if VELOCITIES[m][column] == 1])
        back = tree_sum([f[m] for m in range(19) if VELOCITIES[m][column] == -1])
        components.append((ahead - back) * inverse)
    return density, inverse, components


def dot(vector, u):
    total = None
    for c, x in zip(vector, u):
        if c == 0:
            continue
        if total is None:
            total = x if c == 1 else -x
        else:
            total = total + x if c == 1 else total - x
    return total


def collide(f, density, u, fluid):
    base = 1.0 - 1.5 * (u[0] * u[0] + u[1] * u[1] + u[2] * u[2])
    keep = 1.0 - 1.0 / RELAX_TIME
    scaled = density * (1.0 / RELAX_TIME)
    heavy = scaled * (1.0 / 18.0)
    light = scaled * (1.0 / 36.0)
    post = [None] * 19
    post[0] = jnp.where(fluid, scaled * (1.0 / 3.0) * base + keep * f[0], f[0])
    for m in range(1, 19, 2):
        weight = heavy if m < 7 else light
        projected = dot(VELOCITIES[m], u)
        even = weight * (base + 4.5 * (projected * projected))
        odd = (3.0 * weight) * projected
        post[m] = jnp.where(fluid, (even + odd) + keep * f[m], f[m + 1])
        post[m + 1] = jnp.where(fluid, (even - odd) + keep * f[m + 1], f[m])
    return post


def split(x):
    high = x.astype(jnp.bfloat16)
    low = (x - high.astype(jnp.float32)).astype(jnp.bfloat16)
    return high, low


def product(x, w_high, w_low, dims):
    high, low = split(x)
    one = functools.partial(
        lax.dot_general, dimension_numbers=(dims, ((), ())), preferred_element_type=jnp.float32
    )
    return one(high, w_high) + (one(low, w_high) + one(high, w_low))


def edge(value, packed, vector):
    j = EDGES.index(vector)
    lane = lax.broadcasted_iota(jnp.int32, value.shape, 1)
    if vector[2] == 1:
        there = packed if j == 0 else pltpu.roll(packed, 128 - j, 1)
        return jnp.where(lane == 0, there, value)
    return jnp.where(lane == 127, pltpu.roll(packed, 127 - j, 1), value)


def unpacked(packed, rb):
    return pltpu.roll(packed, lax.rem(128 - SPAN * rb, 128), 1)


def patch(pb, er, pp):
    def block(rb, carry):
        row = pl.multiple_of(rb * SIZE + 8, 8)
        packed = unpacked(er[0], rb)
        for k, vector in enumerate(DIAGONAL):
            value = pb[INPLANE.index(vector), pl.ds(row, SIZE), :]
            pp[k, pl.ds(row, SIZE), :] = edge(value, packed, vector)
        return carry

    lax.fori_loop(0, BLOCKS, block, 0, unroll=True)
    before = pltpu.roll(er[1, SIZE - 8 :, :], SPAN, 1)
    after = er[2, 0:8, :]
    for k, vector in enumerate(DIAGONAL):
        packed, row = (before, 0) if vector[1] == 1 else (after, 72)
        value = pb[INPLANE.index(vector), pl.ds(row, 8), :]
        pp[k, pl.ds(row, 8), :] = edge(value, packed, vector)


def streamed(pb, zr, er, pp, rb):
    row = pl.multiple_of(rb * SIZE, 8)
    packed = {0: unpacked(er[0], rb), 1: unpacked(er[3], rb), -1: unpacked(er[4], rb)}
    f = []
    for vector in VELOCITIES:
        rows = pl.ds(row + (8 - vector[1]), SIZE)
        if vector in DIAGONAL:
            f.append(pp[DIAGONAL.index(vector), rows, :])
            continue
        if vector[0] == 0:
            value = pb[INPLANE.index(vector), rows, :]
        else:
            way = 0 if vector[0] == 1 else 1
            value = zr[way, AXIAL[way].index(vector), rows, :]
        if vector[2] != 0:
            value = edge(value, packed[vector[0]], vector)
        f.append(value)
    return f


def kernel(
    gz_size,
    pops_in,
    solid_in,
    whirl_in,
    cells_in,
    weights_in,
    target_in,
    pb_last,
    zr_last,
    er_last,
    force_last,
    pb_early,
    zs,
    zr_early,
    es,
    er_early,
    pp,
    st,
    mom,
    fb,
    mk_own,
    mk_all,
    mk,
    sp,
    wx,
    wy_high,
    wy_low,
    send_sem,
    recv_sem,
    mk_send,
    mk_recv,
    pops,
    solid,
    whirl,
    cells,
    weights,
    target,
    strip_out,
    strip_in,
    rows_in,
    full,
    load_sem,
    vouch_sem,
):
    loads = [
        pltpu.make_async_copy(src, dst, load_sem.at[k])
        for k, (src, dst) in enumerate(
            [
                (cells_in, cells),
                (weights_in, weights),
                (target_in, target),
                (whirl_in, whirl),
                (pops_in, pops),
                (solid_in, solid),
            ]
        )
    ]
    for load in loads:
        load.start()
    pb = [pb_early.at[s] for s in range(STEPS - 1)] + [pb_last]
    zr = [zr_early.at[s] for s in range(STEPS - 1)] + [zr_last]
    er = [er_early.at[s] for s in range(STEPS - 1)] + [er_last]
    gz = lax.axis_index("gz")
    gx = lax.axis_index("gx")
    gy = lax.axis_index("gy")
    z_next, z_prev = lax.rem(gz + 1, gz_size), lax.rem(gz + gz_size - 1, gz_size)
    x_next, x_prev, x_far = lax.rem(gx + 1, 4), lax.rem(gx + 3, 4), lax.rem(gx + 2, 4)
    y_other = 1 - gy
    flip = gx // 2
    is_centre = lax.rem((gx + 1) // 2, 2)
    centre = is_centre == 1
    outer = is_centre == 0
    quarter = lax.rem(2 * gx + gy + 2, 4)
    own = 2 * gx + gy
    beside_y = 2 * (quarter // 2) + 1 - gy
    beside_x = 2 * (1 - quarter // 2) + gy
    outer_start = pl.multiple_of(CENTRE_ROWS * flip, 8)
    centre_start = pl.multiple_of(OUTER_ROWS * (1 - flip), 8)

    barrier = pltpu.get_barrier_semaphore()
    neighbours = [
        {"gz": gz, "gx": x_next, "gy": gy},
        {"gz": gz, "gx": x_prev, "gy": gy},
        {"gz": gz, "gx": x_far, "gy": gy},
        {"gz": gz, "gx": gx, "gy": y_other},
        {"gz": gz, "gx": x_next, "gy": y_other},
        {"gz": gz, "gx": x_prev, "gy": y_other},
        {"gz": gz, "gx": x_far, "gy": y_other},
    ]
    for z in (z_next, z_prev):
        neighbours.append({"gz": z, "gx": gx, "gy": gy})
    for place in neighbours:
        pl.semaphore_signal(barrier, inc=1, device_id=place, device_id_type=MESH)

    lanes = lax.broadcasted_iota(jnp.int32, (SIZE, 128), 1)
    lane_block = lanes // SPAN

    def block_of(b):
        return b + flip * (BLOCKS - 1 - 2 * b)

    def remote(src, dst, s, n, place, n_recv=None):
        return pltpu.make_async_remote_copy(
            src_ref=src,
            dst_ref=dst,
            send_sem=send_sem.at[s, n],
            recv_sem=recv_sem.at[s, n if n_recv is None else n_recv],
            device_id=place,
            device_id_type=MESH,
        )

    def axial(s, way, part):
        start, size = ((outer_start, OUTER_ROWS), (centre_start, CENTRE_ROWS))[part]
        return remote(
            zs.at[s, way, :, pl.ds(start, size), :],
            zr[s].at[way, :, pl.ds(pl.multiple_of(start + 8, 8), size), :],
            s,
            N_AXIAL + 2 * way + part,
            {"gz": (z_next, z_prev)[way], "gx": gx, "gy": gy},
        )

    def small(s):
        copies = []
        for way in range(2):
            z = (z_next, z_prev)[way]
            copies.append(
                remote(
                    zs.at[s, way, 3, pl.ds(56, 8), :],
                    zr[s].at[way, 3, pl.ds(0, 8), :],
                    s,
                    N_AXIAL_ROW + 2 * way,
                    {"gz": z, "gx": x_next, "gy": gy},
                )
            )
            copies.append(
                remote(
                    zs.at[s, way, 4, pl.ds(0, 8), :],
                    zr[s].at[way, 4, pl.ds(72, 8), :],
                    s,
                    N_AXIAL_ROW + 2 * way + 1,
                    {"gz": z, "gx": x_prev, "gy": gy},
                )
            )
        copies.append(
            remote(
                pb[s].at[pl.ds(3, 3), pl.ds(64, 8), :],
                pb[s].at[pl.ds(3, 3), pl.ds(0, 8), :],
                s,
                N_ROW,
                {"gz": gz, "gx": x_next, "gy": gy},
            )
        )
        copies.append(
            remote(
                pb[s].at[pl.ds(6, 3), pl.ds(8, 8), :],
                pb[s].at[pl.ds(6, 3), pl.ds(72, 8), :],
                s,
                N_ROW + 1,
                {"gz": gz, "gx": x_prev, "gy": gy},
            )
        )
        places = [
            {"gz": gz, "gx": gx, "gy": y_other},
            {"gz": gz, "gx": x_next, "gy": y_other},
            {"gz": gz, "gx": x_prev, "gy": y_other},
            {"gz": z_next, "gx": gx, "gy": y_other},
            {"gz": z_prev, "gx": gx, "gy": y_other},
        ]
        for k, place in enumerate(places):
            copies.append(remote(es.at[s], er[s].at[k], s, N_EDGE + k, place))
        return copies

    def sample_copies(s):
        pair = 3 - gx
        places = [(gx, y_other), (pair, gy)]
        if s == STEPS - 1:
            places += [(pair, y_other), (0, gy), (0, y_other), (3, gy), (3, y_other)]
        return [
            remote(
                sp.at[s, quarter],
                sp.at[s, quarter],
                s,
                N_SAMPLE + d,
                {"gz": gz, "gx": x, "gy": y},
                N_SAMPLE + quarter,
            )
            for d, (x, y) in enumerate(places)
        ]

    def sample_wait(s, q):
        remote(sp.at[s, q], sp.at[s, q], s, N_SAMPLE, neighbours[0], N_SAMPLE + q).wait_recv()

    def strip_copies():
        edge_rows = pl.ds(pl.multiple_of(56 - 56 * flip, 8), 8)
        return [
            remote(
                mom.at[pl.ds(0, 3), edge_rows, :],
                rows_in,
                0,
                N_STRIP,
                {"gz": gz, "gx": 3 - gx, "gy": gy},
            ),
            remote(strip_out, strip_in, 0, N_STRIP + 1, {"gz": gz, "gx": gx, "gy": y_other}),
        ]

    def centre_place(t):
        return {"gz": gz, "gx": 1 + t // 2, "gy": t % 2}

    def marker_copy(t):
        return pltpu.make_async_remote_copy(
            src_ref=mk_all.at[own],
            dst_ref=mk_all.at[own],
            send_sem=mk_send.at[t],
            recv_sem=mk_recv.at[own],
            device_id=centre_place(t),
            device_id_type=MESH,
        )

    def marker_wait(j):
        pltpu.make_async_remote_copy(
            src_ref=mk_all.at[j],
            dst_ref=mk_all.at[j],
            send_sem=mk_send.at[0],
            recv_sem=mk_recv.at[j],
            device_id=neighbours[0],
            device_id_type=MESH,
        ).wait_recv()

    def not_self(t):
        return jnp.logical_or(gx != 1 + t // 2, gy != t % 2)

    def gather(s, rb):
        if s == 0:
            row = pl.multiple_of(rb * SIZE, 8)
            return [pops[m, 0, pl.ds(row, SIZE), :] for m in range(19)]
        return streamed(pb[s - 1], zr[s - 1], er[s - 1], pp, rb)

    def store_post(s, rb, post):
        row = pl.multiple_of(rb * SIZE, 8)
        for vector in VELOCITIES:
            value = post[INDEX[vector]]
            if vector[2] != 0:
                value = pltpu.roll(value, 1 if vector[2] == 1 else 127, 1)
            if vector[0] == 0:
                pb[s][INPLANE.index(vector), pl.ds(pl.multiple_of(row + 8, 8), SIZE), :] = value
            else:
                way = 0 if vector[0] == 1 else 1
                zs[s, way, AXIAL[way].index(vector), pl.ds(row, SIZE), :] = value
        packed = post[INDEX[EDGES[0]]]
        packed = pltpu.roll(packed, 1, 1)
        for j, vector in enumerate(EDGES):
            if j == 0:
                continue
            shift = j + 1 if vector[2] == 1 else j
            packed = jnp.where(lanes == j, pltpu.roll(post[INDEX[vector]], shift, 1), packed)
        es[s] = jnp.where(lane_block == rb, pltpu.roll(packed, SPAN * rb, 1), es[s])

    def fluid_of(rb):
        return solid[0, pl.ds(pl.multiple_of(rb * SIZE, 8), SIZE), :] == 0

    def whole_block(s):
        def block(b, carry):
            rb = block_of(b)
            f = gather(s, rb)
            density, _, u = moments(f)
            store_post(s, rb, collide(f, density, u, fluid_of(rb)))
            return carry

        return block

    def first_half(s):
        def block(b, carry):
            rb = block_of(b)
            row = pl.multiple_of(rb * SIZE, 8)
            f = gather(s, rb)
            density, inverse, u = moments(f)
            if s > 0:
                for m in range(19):
                    st[m, pl.ds(row, SIZE), :] = f[m]
            for c, value in enumerate([*u, density, inverse]):
                mom[c, pl.ds(row, SIZE), :] = value
            return carry

        return block

    def second_half(s):
        def block(b, carry):
            rb = block_of(b)
            row = pl.multiple_of(rb * SIZE, 8)
            if s == 0:
                f = [pops[m, 0, pl.ds(row, SIZE), :] for m in range(19)]
            else:
                f = [st[m, pl.ds(row, SIZE), :] for m in range(19)]
            density = mom[3, pl.ds(row, SIZE), :]
            scale = RELAX_TIME * mom[4, pl.ds(row, SIZE), :]
            near = pl.multiple_of(row - centre_start, 8)
            u = [mom[c, pl.ds(row, SIZE), :] + scale * fb[c, pl.ds(near, SIZE), :] for c in range(3)]
            store_post(s, rb, collide(f, density, u, fluid_of(rb)))
            return carry

        return block

    def matrix(s, size, first, dim):
        base = mk[dim : dim + 1, :] + (127 + whirl[dim, s]).astype(jnp.float32)
        place = lax.broadcasted_iota(jnp.int32, (size, 256), 0) + first
        distance = place.astype(jnp.float32) - base
        result = jnp.zeros((size, 256), jnp.float32)
        for a in range(4):
            row = 2 + 4 * dim + a
            result = jnp.where(distance == float(a), mk[row : row + 1, :], result)
        return result

    def marker_matrices(s):
        wx[...] = matrix(s, CENTRE_ROWS, 64 * gx + centre_start, 0)
        high, low = split(matrix(s, 128, 128 * gy, 1))
        wy_high[...] = high
        wy_low[...] = low

    def sample(s):
        u = mom[0:3, pl.ds(centre_start, CENTRE_ROWS), :].reshape(3 * CENTRE_ROWS, 128)
        along = product(u, wy_high[...], wy_low[...], ((1,), (0,)))
        spread = wx[...]
        rows = [
            jnp.sum(along[c * CENTRE_ROWS : (c + 1) * CENTRE_ROWS] * spread, axis=0, keepdims=True)
            for c in range(3)
        ]
        sp[s, quarter] = jnp.concatenate(rows + [jnp.zeros((5, 256), jnp.float32)], axis=0)

    def pack_strips():
        packed = jnp.zeros((SIZE, 128), jnp.float32)
        for c in range(3):
            for b in range(CENTRE_BLOCKS):
                value = mom[c, pl.ds(pl.multiple_of(centre_start + SIZE * b, 8), SIZE), :]
                first = 4 * (CENTRE_BLOCKS * c + b)
                value = pltpu.roll(value, first + 4 * (1 - gy), 1)
                packed = jnp.where((lanes >= first) & (lanes < first + 4), value, packed)
        strip_out[...] = packed

    def sample_full():
        u = mom[0:3, pl.ds(centre_start, CENTRE_ROWS), :].reshape(3 * CENTRE_ROWS, 128)
        beside = rows_in[...].reshape(24, 128)
        along = product(
            jnp.concatenate([u, beside], axis=0), wy_high[...], wy_low[...], ((1,), (0,))
        )
        spread = wx[...]
        spread_beside = matrix(0, 8, 64 * gx + 64 - 72 * flip, 0)
        wanted = jnp.where(gy == 0, lanes, 127 - lanes) < 4
        packed = strip_in[...]
        pieces = []
        for c in range(3):
            for b in range(CENTRE_BLOCKS):
                shift = lax.rem(256 - 4 * (CENTRE_BLOCKS * c + b) - 4 * gy, 128)
                pieces.append(jnp.where(wanted, pltpu.roll(packed, shift, 1), 0.0))
        across = product(
            jnp.concatenate(pieces, axis=0), *split(matrix(0, 128, 128 * (1 - gy), 1)), ((1,), (0,))
        )
        rows = []
        for c in range(3):
            part = slice(c * CENTRE_ROWS, (c + 1) * CENTRE_ROWS)
            first = 3 * CENTRE_ROWS + 8 * c
            total = jnp.sum((along[part] + across[part]) * spread, axis=0, keepdims=True)
            total += jnp.sum(along[first : first + 8] * spread_beside, axis=0, keepdims=True)
            rows.append(total)
        full[...] = jnp.concatenate(rows, axis=0)

    def near_sampled(s):
        return sp[s, quarter] + (sp[s, beside_y] + sp[s, beside_x])

    def sampled(s):
        return (sp[s, 0] + sp[s, 1]) + (sp[s, 2] + sp[s, 3])

    def force(s):
        push = mk[10:13, :] - (full[...] if s == 0 else near_sampled(s)[0:3, :])
        spread = wx[...]
        weighted = jnp.concatenate([spread * push[c : c + 1, :] for c in range(3)], axis=0)
        body = product(weighted, wy_high[...], wy_low[...], ((1,), (1,)))
        fb[...] = body.reshape(3, CENTRE_ROWS, 128)

    for load in loads[:4]:
        load.wait()
    mk_own[...] = jnp.zeros((16, 128), jnp.float32)
    mk_own[0:2, 0:32] = cells[:, 0, :].astype(jnp.float32)
    mk_own[2:6, 0:32] = weights[0, :, 0, :]
    mk_own[6:10, 0:32] = weights[1, :, 0, :]
    mk_own[10:13, 0:32] = target[:, 0, :]
    mk_all[own] = pltpu.roll(mk_own[...], 32 * lax.rem(own, 4), 1)

    pl.semaphore_wait(barrier, len(neighbours))
    for t in range(4):

        @pl.when(not_self(t))
        def _(t=t):
            marker_copy(t).start()

    vouched = [neighbours[0], neighbours[1], neighbours[3]]
    for place in vouched:
        pl.semaphore_signal(vouch_sem, inc=1, device_id=place, device_id_type=MESH)

    for load in loads[4:]:
        load.wait()

    for s in range(STEPS):
        last = s == STEPS - 1
        if s > 0:
            for copy in [axial(s - 1, way, part) for way in range(2) for part in range(2)] + small(s - 1):
                copy.wait_recv()
            patch(pb[s - 1], er[s - 1], pp)

        @pl.when(centre)
        def _(s=s):
            if s == 1:
                for copy in strip_copies():
                    copy.wait_send()
            lax.fori_loop(OUTER_BLOCKS, BLOCKS, first_half(s), 0, unroll=True)
            if s == 0:
                pack_strips()
                for copy in strip_copies():
                    copy.start()
            else:
                sample(s)
                for copy in sample_copies(s):
                    copy.start()

        lax.fori_loop(0, OUTER_BLOCKS, whole_block(s), 0, unroll=True)
        for way in range(2):
            axial(s, way, 0).start()

        @pl.when(outer)
        def _(s=s):
            lax.fori_loop(OUTER_BLOCKS, BLOCKS, whole_block(s), 0, unroll=True)

        @pl.when(centre)
        def _(s=s):
            if s == 0:
                for d in range(1, 8):
                    marker_wait(lax.rem(own + d, 8))
                mk[:, 0:128] = (mk_all[0] + mk_all[1]) + (mk_all[2] + mk_all[3])
                mk[:, 128:256] = (mk_all[4] + mk_all[5]) + (mk_all[6] + mk_all[7])
                marker_matrices(s)
                for copy in strip_copies():
                    copy.wait_recv()
                sample_full()
            else:
                sample_wait(s, beside_y)
                sample_wait(s, beside_x)
                if s == STEPS - 1:
                    sample_wait(s, 3 - quarter)
            force(s)
            lax.fori_loop(OUTER_BLOCKS, BLOCKS, second_half(s), 0, unroll=True)

        if s == 0:
            pl.semaphore_wait(vouch_sem, len(vouched))
        for copy in small(s)[::-1]:
            copy.start()
        for way in range(2):
            axial(s, way, 1).start()

        if not last:

            @pl.when(centre)
            def _(s=s):
                marker_matrices(s + 1)

    @pl.when(outer)
    def _():
        for q in range(4):
            sample_wait(STEPS - 1, q)

    total = sampled(STEPS - 1)
    half = jnp.where(own // 4 == 0, total[:, 0:128], total[:, 128:256])
    half = pltpu.roll(half, lax.rem(128 - 32 * lax.rem(own, 4), 128), 1)
    force_last[:, 0, :] = (target[:, 0, :] - half[0:3, 0:32]) * (1.0 / SPEED_SCALE)

    for t in range(4):

        @pl.when(not_self(t))
        def _(t=t):
            marker_copy(t).wait_send()

    @pl.when(centre)
    def _():
        for s in range(1, STEPS):
            for copy in sample_copies(s):
                copy.wait_send()

    for s in range(STEPS):
        for copy in small(s) + [axial(s, way, part) for part in range(2) for way in range(2)]:
            copy.wait_send()

    for copy in small(STEPS - 1)[::-1] + [
        axial(STEPS - 1, way, part) for part in range(2) for way in range(2)
    ]:
        copy.wait_recv()


def finish(pb, zr, er, force, solid, res_pops, res_vel, res_force, pp, out_pops, out_vel, sem):
    patch(pb, er, pp)
    copies = []
    for rb in range(BLOCKS):
        rows = pl.ds(rb * SIZE, SIZE)
        f = streamed(pb, zr, er, pp, rb)
        for m in range(19):
            out_pops[m, 0, rows, :] = f[m]
        _, _, u = moments(f)
        fluid = solid[0, rows, :] == 0
        for c in range(3):
            out_vel[c, 0, rows, :] = jnp.where(fluid, u[c] * (1.0 / SPEED_SCALE), 0.0)
        for k, (src, dst) in enumerate([(out_pops, res_pops), (out_vel, res_vel)]):
            copy = pltpu.make_async_copy(
                src.at[:, :, rows, :], dst.at[:, :, rows, :], sem.at[2 * rb + k]
            )
            copy.start()
            copies.append(copy)
    copy = pltpu.make_async_copy(force, res_force, sem.at[2 * BLOCKS])
    copy.start()
    copies.append(copy)
    for copy in copies:
        copy.wait()


def body(populations, solid_mask, whirl_offsets, marker_cells, marker_weights, pipe_velocity):
    f32 = jnp.float32
    vmem = pl.BlockSpec(memory_space=pltpu.VMEM)
    hbm = pl.BlockSpec(memory_space=pltpu.HBM)
    pb, zr, er = (9, 80, 128), (2, 5, 80, 128), (5, SIZE, 128)
    arrived = pl.pallas_call(
        functools.partial(kernel, lax.axis_size("gz")),
        out_shape=[pltpu.VMEM(shape, f32) for shape in (pb, zr, er, pipe_velocity.shape)],
        in_specs=[hbm] * 6,
        out_specs=[vmem] * 4,
        scratch_shapes=[
            pltpu.VMEM((STEPS - 1,) + pb, f32),
            pltpu.VMEM((STEPS, 2, 5, 64, 128), f32),
            pltpu.VMEM((STEPS - 1,) + zr, f32),
            pltpu.VMEM((STEPS, SIZE, 128), f32),
            pltpu.VMEM((STEPS - 1,) + er, f32),
            pltpu.VMEM((4, 80, 128), f32),
            pltpu.VMEM((19, 64, 128), f32),
            pltpu.VMEM((5, 64, 128), f32),
            pltpu.VMEM((3, CENTRE_ROWS, 128), f32),
            pltpu.VMEM((16, 128), f32),
            pltpu.VMEM((8, 16, 128), f32),
            pltpu.VMEM((16, 256), f32),
            pltpu.VMEM((STEPS, 4, 8, 256), f32),
            pltpu.VMEM((CENTRE_ROWS, 256), f32),
            pltpu.VMEM((128, 256), jnp.bfloat16),
            pltpu.VMEM((128, 256), jnp.bfloat16),
            pltpu.SemaphoreType.DMA((STEPS, N_MESSAGES)),
            pltpu.SemaphoreType.DMA((STEPS, N_MESSAGES)),
            pltpu.SemaphoreType.DMA((4,)),
            pltpu.SemaphoreType.DMA((8,)),
            pltpu.VMEM(populations.shape, f32),
            pltpu.VMEM(solid_mask.shape, jnp.int32),
            pltpu.SMEM(whirl_offsets.shape[::-1], jnp.int32),
            pltpu.VMEM(marker_cells.shape, jnp.int32),
            pltpu.VMEM(marker_weights.shape, f32),
            pltpu.VMEM(pipe_velocity.shape, f32),
            pltpu.VMEM((SIZE, 128), f32),
            pltpu.VMEM((SIZE, 128), f32),
            pltpu.VMEM((3, 8, 128), f32),
            pltpu.VMEM((3, 256), f32),
            pltpu.SemaphoreType.DMA((6,)),
            pltpu.SemaphoreType.REGULAR,
        ],
        compiler_params=pltpu.CompilerParams(
            collective_id=0, has_side_effects=True, vmem_limit_bytes=60 * 1024 * 1024
        ),
        cost_estimate=pl.CostEstimate(flops=40_000_000, bytes_accessed=2_000_000, transcendentals=0),
    )(populations, solid_mask, whirl_offsets.T, marker_cells, marker_weights, pipe_velocity)
    shapes = (populations.shape, (3,) + solid_mask.shape, pipe_velocity.shape)
    return pl.pallas_call(
        finish,
        out_shape=[jax.ShapeDtypeStruct(shape, f32) for shape in shapes],
        in_specs=[vmem] * 5,
        out_specs=[hbm] * 3,
        scratch_shapes=[pltpu.VMEM((4, 80, 128), f32)]
        + [pltpu.VMEM(shape, f32) for shape in shapes[:2]]
        + [pltpu.SemaphoreType.DMA((2 * BLOCKS + 1,))],
        compiler_params=pltpu.CompilerParams(vmem_limit_bytes=24 * 1024 * 1024),
        cost_estimate=pl.CostEstimate(flops=2_000_000, bytes_accessed=2_000_000, transcendentals=0),
    )(*arrived, solid_mask)


def solution(mesh):
    in_specs = (
        P(None, "gz", "gx", "gy"),
        P("gz", "gx", "gy"),
        P(),
        P(None, "gz", ("gx", "gy")),
        P(None, None, "gz", ("gx", "gy")),
        P(None, "gz", ("gx", "gy")),
    )
    out_specs = (P(None, "gz", "gx", "gy"), P(None, "gz", "gx", "gy"), P(None, "gz", ("gx", "gy")))
    return jax.shard_map(body, mesh=mesh, in_specs=in_specs, out_specs=out_specs, check_vma=False)
```
